256 devices in a mesh: seq: 32 (over x, z_lo, core), dp: 8 (over y, z_hi).
Axes of the slice: x: 4, y: 4, z: 8 (z_hi: 2, z_lo: 4; z = z_hi * 4 + z_lo), core: 2. Of those that a mesh axis runs over, the one named last changes fastest.
Arguments:
- activations: bfloat16 [8, 32768, 256], P('dp', 'seq'), may hold values from -6 to 6
- gate_values: bfloat16 [8, 32768, 256], P('dp', 'seq'), may hold values from -6 to 6
- output_grad: bfloat16 [8, 32768, 256], P('dp', 'seq'), may hold values from -6 to 6
- filter_codes: bfloat16 [32768, 256], P('seq'), may hold values from -4 to 4
- filter_scales: float32 [256, 256], P('seq'), as said below
Outputs:
- input_grad: float32 [8, 32768, 256], P('dp', 'seq')
- gate_grad: bfloat16 [8, 32768, 256], P('dp', 'seq')
- code_grad: float32 [32768, 256], P('seq')
The draws below stay inside these ranges and needn't reach their ends.
Inputs may be any that keep to these rules, and one draw needn't show every extreme that they name: `filter_scales`: every entry lies between 0.3 / sqrt(32768) and 3 / sqrt(32768).
All inputs are finite; a program needn't handle non-finite values.
Results may differ from the reference program's by a relative error of at most 0.001.
Values may be sent and summed in bfloat16 or wider, within the bound.
A program may use at most 128 MiB of HBM per device.

```python
import math
import jax
import jax.numpy as jnp
from jax import lax

C = 256
QBLOCK = 128
LEN = 32768
REPL = 8


def draw_filter_scales(key, part):
    key = jax.random.fold_in(key, 7)
    factor = jnp.exp(jax.random.uniform(key, (LEN // QBLOCK, C), jnp.float32, math.log(0.3), math.log(3.0)))
    return factor / math.sqrt(LEN)


def block_levels(key, extent, pieces, low, high):
    gain, own = 1.0, jax.random.fold_in(key, 6)
    for dim, shards_of in pieces:
        steps = jnp.exp(jax.random.uniform(jax.random.fold_in(own, dim), (shards_of,), jnp.float32, low / len(pieces), high / len(pieces)))
        gain = gain * jnp.repeat(steps, extent[dim] // shards_of).reshape([-1 if axis == dim else 1 for axis in range(len(extent))])
    return gain


def centred(rng, shape, deviation, bound, pieces=(), kind=jnp.bfloat16):
    values = jax.random.normal(rng, shape, jnp.float32) * deviation
    if len(pieces) > 0:
        values = block_levels(rng, shape, pieces, -0.22, 0.18) * values
    return jnp.clip(values, min=-bound, max=bound).astype(kind)


def setup_inputs(seed: int = 0) -> dict:
    key_list = jax.random.split(jax.random.key(seed), 6)
    activations = centred(key_list[0], (REPL, LEN, C), 1.0, 6.0, ((0, 8), (1, 32)))
    gate_values = centred(key_list[1], (REPL, LEN, C), 1.0, 6.0, ((0, 8), (1, 32)))
    output_grad = centred(key_list[2], (REPL, LEN, C), 1.0, 6.0, ((0, 8), (1, 32)))
    filter_codes = centred(key_list[3], (LEN, C), 1.0, 4.0, ((0, 32),))
    filter_scales = draw_filter_scales(jax.random.fold_in(key_list[5], 71), 0)
    return {"activations": activations, "gate_values": gate_values, "output_grad": output_grad, "filter_codes": filter_codes, "filter_scales": filter_scales}


def reference(activations, gate_values, output_grad, filter_codes, filter_scales):
    length = activations.shape[1]
    padded_len = 2 * length
    scale_rows = jnp.repeat(filter_scales, QBLOCK, axis=0)
    filter_taps = filter_codes.astype(jnp.float32) * scale_rows
    taps_spec = jnp.fft.rfft(filter_taps, n=padded_len, axis=0)

    def replica(operands):
        tokens_in, gate_in, grad_in = operands
        signal = tokens_in.astype(jnp.float32)
        grad_full = grad_in.astype(jnp.float32)
        grad_act = grad_full * gate_in.astype(jnp.float32)
        signal_spec = jnp.fft.rfft(signal, n=padded_len, axis=0)
        act_spec = jnp.fft.rfft(grad_act, n=padded_len, axis=0)
        conv_out = jnp.fft.irfft(signal_spec * taps_spec, n=padded_len, axis=0)[:length]
        back_grad = jnp.fft.irfft(act_spec * jnp.conj(taps_spec), n=padded_len, axis=0)[:length]
        taps_grad = jnp.fft.irfft(act_spec * jnp.conj(signal_spec), n=padded_len, axis=0)[:length]
        gate_out = (grad_full * conv_out).astype(jnp.bfloat16)
        return back_grad, gate_out, taps_grad

    input_grad, gate_grad, taps_grads = lax.map(replica, (activations, gate_values, output_grad))
    code_grad = jnp.sum(taps_grads, axis=0) * scale_rows
    return input_grad, gate_grad, code_grad
```

```python
import math

import jax
import jax.numpy as jnp
import numpy as np
from jax import lax
from jax.experimental import pallas as pl
from jax.experimental.pallas import tpu as pltpu
from jax.sharding import PartitionSpec as P

BOTH = ("seq", "dp")
LANES = 128
SUB = 8
ROWS = 256
FLOOR = 2.0**-90
TOP8 = 2.0**15
TOP16 = 2.0**7.5


def split_np(table):
    high = np.asarray(table, np.float64).astype(jnp.bfloat16)
    low = (np.asarray(table, np.float64) - high.astype(np.float64)).astype(jnp.bfloat16)
    return high, low


def tables():
    whole = 2 * ROWS * LANES
    rows = np.arange(ROWS, dtype=np.float64)
    lanes = np.arange(LANES, dtype=np.float64)
    outer = 2 * np.pi * (rows[:, None] + 0.5) * rows[None, :] / (2 * ROWS)
    first = np.concatenate([np.cos(outer), -np.sin(outer)], axis=0)
    last = np.concatenate([np.cos(outer.T), -np.sin(outer.T)], axis=1) * (2.0 / whole)
    inner = 2 * np.pi * lanes[:, None] * lanes[None, :] / LANES
    cos, sin = np.cos(inner), np.sin(inner)
    forward = np.block([[cos, -sin], [sin, cos]])
    backward = np.block([[cos, sin], [-sin, cos]])
    turn = 2 * np.pi * (rows[:, None] + 0.5) * lanes[None, :] / whole
    twist = np.stack([np.cos(turn), -np.sin(turn)]).astype(np.float32)
    first_hi, first_lo = split_np(first)
    last_hi, last_lo = split_np(last)
    return (
        np.concatenate([first_hi, first_lo], axis=0),
        np.concatenate([last_hi, last_lo], axis=0),
        np.stack(split_np(forward)),
        np.stack(split_np(backward)),
        twist,
    )


def dot(left, right):
    return jnp.dot(left, right, preferred_element_type=jnp.float32)


def halves(value):
    high = value.astype(jnp.bfloat16)
    low = (value - high.astype(jnp.float32)).astype(jnp.bfloat16)
    return high, low


def left_product(table_ref, high, low):
    count = table_ref.shape[0] // 2
    both = dot(table_ref[...], high)
    total = both[:count] + both[count:]
    if low is not None:
        total = total + dot(table_ref[:count], low)
    return total


def right_product(value, table_ref):
    high, low = halves(value)
    return dot(high, table_ref[0]) + dot(low, table_ref[0]) + dot(high, table_ref[1])


def forward(high, low, first_ref, forward_ref, twist_ref):
    section = left_product(first_ref, high, low)
    cos, sin = twist_ref[0], twist_ref[1]
    out = []
    for start in range(0, high.shape[1], LANES):
        real = section[:ROWS, start : start + LANES]
        imag = section[ROWS:, start : start + LANES]
        turned = jnp.concatenate([real * cos - imag * sin, real * sin + imag * cos], axis=1)
        out.append(right_product(turned, forward_ref))
    return out


def inverse(spectra, last_ref, backward_ref, twist_ref):
    cos, sin = twist_ref[0], twist_ref[1]
    sections = []
    for spec in spectra:
        part = right_product(spec, backward_ref)
        real, imag = part[:, :LANES], part[:, LANES:]
        sections.append(jnp.concatenate([real * cos + imag * sin, imag * cos - real * sin], axis=0))
    high, low = halves(jnp.concatenate(sections, axis=1))
    result = left_product(last_ref, high, low)
    return [result[:, i * LANES : (i + 1) * LANES] for i in range(len(spectra))]


def times(left, right):
    lr, li, rr, ri = left[:, :LANES], left[:, LANES:], right[:, :LANES], right[:, LANES:]
    return jnp.concatenate([lr * rr - li * ri, lr * ri + li * rr], axis=1)


def times_conj(left, right):
    lr, li, rr, ri = left[:, :LANES], left[:, LANES:], right[:, :LANES], right[:, LANES:]
    return jnp.concatenate([lr * rr + li * ri, li * rr - lr * ri], axis=1)


def eighth_power(value):
    two = value * value
    four = two * two
    return four * two * value * jnp.abs(value)


def sixteenth_power(value):
    two = value * value
    four = two * two
    return four * four * four * two * value * jnp.abs(value)


def root_of(code, steps):
    size = jnp.exp2(jnp.log2(jnp.abs(code)) * (1.0 / 2**steps))
    return jnp.where(code < 0, -size, size)


def transform_kernel(scale_ref, data_ref, taps_ref, first_ref, last_ref, forward_ref, backward_ref, twist_ref,
                     out_ref, out_scale_ref, grad_ref):
    segments, replicas = data_ref.shape[0], data_ref.shape[1]
    taps_high, taps_low = halves(taps_ref[...])
    (taps_spec,) = forward(taps_high, taps_low, first_ref, forward_ref, twist_ref)

    def pair(step, cross):
        signals, acts = [], []
        for half in range(2):
            index = step * 2 + half
            tile = data_ref[:, index].astype(jnp.float32)
            signals.append(tile[:, :SUB].reshape(ROWS, LANES).astype(jnp.bfloat16))
            rooted = root_of(tile[:, SUB:], 3)
            parts = [rooted[s] * scale_ref[s * replicas + index] for s in range(segments)]
            acts.append(jnp.concatenate(parts, axis=0))
        act_high, act_low = halves(jnp.concatenate(acts, axis=1))
        signal_specs = forward(jnp.concatenate(signals, axis=1), None, first_ref, forward_ref, twist_ref)
        act_specs = forward(act_high, act_low, first_ref, forward_ref, twist_ref)
        for signal_spec, act_spec in zip(signal_specs, act_specs):
            cross = cross + times_conj(act_spec, signal_spec)
        convs = inverse([times(s, taps_spec) for s in signal_specs], last_ref, backward_ref, twist_ref)
        backs = inverse([times_conj(a, taps_spec) for a in act_specs], last_ref, backward_ref, twist_ref)
        for half in range(2):
            index = step * 2 + half
            conv, back = convs[half], backs[half]
            conv_top = jnp.maximum(jnp.max(jnp.abs(conv), keepdims=True), FLOOR)
            back_top = jnp.maximum(jnp.max(jnp.abs(back), keepdims=True), FLOOR)
            conv_code = sixteenth_power(conv * (TOP16 / conv_top)).reshape(segments, SUB, LANES)
            back_code = eighth_power(back * (TOP8 / back_top)).reshape(segments, SUB, LANES)
            out_ref[:, index] = jnp.concatenate([conv_code, back_code], axis=1).astype(jnp.bfloat16)
            out_scale_ref[index] = jnp.concatenate(
                [jnp.broadcast_to(conv_top * (1.0 / TOP16), (1, LANES)), jnp.broadcast_to(back_top * (1.0 / TOP8), (1, LANES))],
                axis=0,
            )
        return cross

    cross = lax.fori_loop(0, replicas // 2, pair, jnp.zeros((ROWS, 2 * LANES), jnp.float32))
    (grad,) = inverse([cross], last_ref, backward_ref, twist_ref)
    grad_ref[...] = grad


def transforms(scales, data, taps):
    segments, replicas = data.shape[0], data.shape[1]
    vmem = pl.BlockSpec(memory_space=pltpu.VMEM)
    return pl.pallas_call(
        transform_kernel,
        out_shape=(
            jax.ShapeDtypeStruct(data.shape, jnp.bfloat16),
            jax.ShapeDtypeStruct((replicas, 2, LANES), jnp.float32),
            jax.ShapeDtypeStruct((ROWS, LANES), jnp.float32),
        ),
        in_specs=[pl.BlockSpec(memory_space=pltpu.SMEM)] + [vmem] * 7,
        out_specs=(vmem, vmem, vmem),
        compiler_params=pltpu.CompilerParams(vmem_limit_bytes=48 << 20),
        cost_estimate=pl.CostEstimate(flops=7_000_000_000, bytes_accessed=5_000_000, transcendentals=500_000),
    )(scales, data, taps, *[jnp.asarray(t) for t in tables()])


def by_channel(value):
    return value.reshape(SUB, LANES, value.shape[-1]).transpose(2, 0, 1)


def by_position(value):
    return value.transpose(1, 2, 0).reshape(SUB * LANES, value.shape[0])


def on_device(activations, gate_values, output_grad, filter_codes, filter_scales):
    channels = filter_codes.shape[1]
    seqs, replicas = lax.axis_size("seq"), lax.axis_size("dp")
    replica = lax.axis_index("dp")
    block_size = filter_codes.shape[0] // filter_scales.shape[0]
    grad_in = output_grad[0].astype(jnp.float32)
    act = grad_in * gate_values[0].astype(jnp.float32)
    top = jnp.maximum(jnp.max(jnp.abs(act)), FLOOR)
    scale_all = lax.all_gather((top * (1.0 / TOP8)).reshape(1), BOTH, tiled=True)
    act_code = eighth_power(act * (TOP8 / top)).astype(jnp.bfloat16)
    sent = jnp.concatenate([by_channel(activations[0]), by_channel(act_code)], axis=1)
    got = lax.all_to_all(sent, BOTH, 0, 0, tiled=True)

    scale_rows = jnp.repeat(filter_scales, block_size, axis=0)
    taps = by_channel(filter_codes.astype(jnp.float32) * scale_rows)
    taps_mine = lax.dynamic_index_in_dim(taps.reshape(seqs, replicas, SUB, LANES), replica, 1, keepdims=False)
    taps_got = lax.all_to_all(taps_mine, "seq", 0, 0, tiled=True)

    out, out_scale, grad = transforms(
        scale_all, got.reshape(seqs, replicas, 2 * SUB, LANES), taps_got.reshape(ROWS, LANES)
    )
    out_scale_all = lax.all_gather(out_scale[:, :, 0], BOTH)
    back = lax.all_to_all(out.reshape(channels, 2 * SUB, LANES), BOTH, 0, 0, tiled=True)
    grad_seq = lax.all_to_all(grad.reshape(seqs, SUB, LANES), "seq", 0, 0, tiled=True)
    grad_all = lax.all_gather(grad_seq, "dp", axis=1).reshape(channels, SUB, LANES)

    my_scale = lax.dynamic_index_in_dim(out_scale_all, replica, 1, keepdims=False)
    back = back.astype(jnp.float32)
    conv = by_position(root_of(back[:, :SUB], 4) * my_scale[:, 0, None, None])
    input_grad = by_position(root_of(back[:, SUB:], 3) * my_scale[:, 1, None, None])
    gate_grad = (grad_in * conv).astype(jnp.bfloat16)
    code_grad = by_position(grad_all) * scale_rows
    return (input_grad[None], gate_grad[None], code_grad)


def solution(mesh):
    in_specs = (
        P("dp", "seq", None),
        P("dp", "seq", None),
        P("dp", "seq", None),
        P("seq", None),
        P("seq", None),
    )
    out_specs = (P("dp", "seq", None), P("dp", "seq", None), P("seq", None))
    return jax.shard_map(on_device, mesh=mesh, in_specs=in_specs, out_specs=out_specs, check_vma=False)
```

```python
import functools

import jax
import jax.numpy as jnp
import numpy as np
from jax import lax
from jax.experimental import pallas as pl
from jax.experimental.pallas import tpu as pltpu
from jax.sharding import PartitionSpec as P

LANES = 128
SUB = 8
ROWS = 256
FLOOR = 2.0**-90
TOP8 = 2.0**15
TOP16 = 2.0**7.5
STRIDE = 37


def split_np(table):
    high = np.asarray(table, np.float64).astype(jnp.bfloat16)
    low = (np.asarray(table, np.float64) - high.astype(np.float64)).astype(jnp.bfloat16)
    return high, low


def tables():
    whole = 2 * ROWS * LANES
    rows = np.arange(ROWS, dtype=np.float64)
    lanes = np.arange(LANES, dtype=np.float64)
    outer = 2 * np.pi * (rows[:, None] + 0.5) * rows[None, :] / (2 * ROWS)
    first = np.concatenate([np.cos(outer), -np.sin(outer)], axis=0)
    last = np.concatenate([np.cos(outer.T), -np.sin(outer.T)], axis=1) * (2.0 / whole)
    inner = 2 * np.pi * lanes[:, None] * lanes[None, :] / LANES
    cos, sin = np.cos(inner), np.sin(inner)
    forward = np.block([[cos, -sin], [sin, cos]])
    backward = np.block([[cos, sin], [-sin, cos]])
    turn = 2 * np.pi * (rows[:, None] + 0.5) * lanes[None, :] / whole
    twist = np.stack([np.cos(turn), -np.sin(turn)]).astype(np.float32)
    first_hi, first_lo = split_np(first)
    last_hi, last_lo = split_np(last)
    return (
        np.concatenate([first_hi, first_lo], axis=0),
        np.concatenate([last_hi, last_lo], axis=0),
        np.stack(split_np(forward)),
        np.stack(split_np(backward)),
        twist,
    )


def dot(left, right):
    return jnp.dot(left, right, preferred_element_type=jnp.float32)


def halves(value):
    high = value.astype(jnp.bfloat16)
    low = (value - high.astype(jnp.float32)).astype(jnp.bfloat16)
    return high, low


def left_product(table_ref, high, low):
    count = table_ref.shape[0] // 2
    both = dot(table_ref[...], high)
    total = both[:count] + both[count:]
    if low is not None:
        total = total + dot(table_ref[:count], low)
    return total


def right_product(value, table_ref):
    high, low = halves(value)
    return dot(high, table_ref[0]) + dot(low, table_ref[0]) + dot(high, table_ref[1])


def forward(high, low, first_ref, forward_ref, twist_ref):
    section = left_product(first_ref, high, low)
    cos, sin = twist_ref[0], twist_ref[1]
    out = []
    for start in range(0, high.shape[1], LANES):
        real = section[:ROWS, start : start + LANES]
        imag = section[ROWS:, start : start + LANES]
        turned = jnp.concatenate([real * cos - imag * sin, real * sin + imag * cos], axis=1)
        out.append(right_product(turned, forward_ref))
    return out


def inverse(spectra, last_ref, backward_ref, twist_ref):
    cos, sin = twist_ref[0], twist_ref[1]
    sections = []
    for spec in spectra:
        part = right_product(spec, backward_ref)
        real, imag = part[:, :LANES], part[:, LANES:]
        sections.append(jnp.concatenate([real * cos + imag * sin, imag * cos - real * sin], axis=0))
    high, low = halves(jnp.concatenate(sections, axis=1))
    result = left_product(last_ref, high, low)
    return [result[:, i * LANES : (i + 1) * LANES] for i in range(len(spectra))]


def times(left, right):
    lr, li, rr, ri = left[:, :LANES], left[:, LANES:], right[:, :LANES], right[:, LANES:]
    return jnp.concatenate([lr * rr - li * ri, lr * ri + li * rr], axis=1)


def times_conj(left, right):
    lr, li, rr, ri = left[:, :LANES], left[:, LANES:], right[:, :LANES], right[:, LANES:]
    return jnp.concatenate([lr * rr + li * ri, li * rr - lr * ri], axis=1)


def eighth_power(value):
    two = value * value
    four = two * two
    return four * two * value * jnp.abs(value)


def sixteenth_power(value):
    two = value * value
    four = two * two
    return four * four * four * two * value * jnp.abs(value)


def root_of(code, steps):
    size = jnp.exp2(jnp.log2(jnp.abs(code)) * (1.0 / 2**steps))
    return jnp.where(code < 0, -size, size)


def transform_kernel(scale_ref, data_ref, taps_ref, first_ref, last_ref, forward_ref, backward_ref, twist_ref,
                     out_ref, grad_ref):
    segments, replicas = data_ref.shape[0], data_ref.shape[1]
    taps_high, taps_low = halves(taps_ref[...])
    (taps_spec,) = forward(taps_high, taps_low, first_ref, forward_ref, twist_ref)

    def pair(step, cross):
        signals, acts = [], []
        for half in range(2):
            index = step * 2 + half
            tile = data_ref[:, index].astype(jnp.float32)
            signals.append(tile[:, :SUB].reshape(ROWS, LANES).astype(jnp.bfloat16))
            rooted = root_of(tile[:, SUB:], 3)
            parts = [rooted[s] * scale_ref[s, pl.ds(index, 1)] for s in range(segments)]
            acts.append(jnp.concatenate(parts, axis=0))
        act_high, act_low = halves(jnp.concatenate(acts, axis=1))
        signal_specs = forward(jnp.concatenate(signals, axis=1), None, first_ref, forward_ref, twist_ref)
        act_specs = forward(act_high, act_low, first_ref, forward_ref, twist_ref)
        for signal_spec, act_spec in zip(signal_specs, act_specs):
            cross = cross + times_conj(act_spec, signal_spec)
        convs = inverse([times(s, taps_spec) for s in signal_specs], last_ref, backward_ref, twist_ref)
        backs = inverse([times_conj(a, taps_spec) for a in act_specs], last_ref, backward_ref, twist_ref)
        for half in range(2):
            index = step * 2 + half
            conv, back = convs[half], backs[half]
            conv_top = jnp.maximum(jnp.max(jnp.abs(conv), keepdims=True), FLOOR)
            back_top = jnp.maximum(jnp.max(jnp.abs(back), keepdims=True), FLOOR)
            conv_code = sixteenth_power(conv * (TOP16 / conv_top)).reshape(segments, SUB, LANES)
            back_code = eighth_power(back * (TOP8 / back_top)).reshape(segments, SUB, LANES)
            out_ref[:, index] = jnp.concatenate([conv_code, back_code], axis=1).astype(jnp.bfloat16)
            lane = lax.broadcasted_iota(jnp.int32, (1, LANES), 1)
            row = jnp.where(lane < LANES // 2, conv_top * (1.0 / TOP16), back_top * (1.0 / TOP8))
            for s in range(segments):
                grad_ref[s, pl.ds(SUB + index, 1)] = row
        return cross

    cross = lax.fori_loop(0, replicas // 2, pair, jnp.zeros((ROWS, 2 * LANES), jnp.float32))
    (grad,) = inverse([cross], last_ref, backward_ref, twist_ref)
    grad_ref[:, :SUB] = grad.reshape(segments, SUB, LANES)


def transforms(scales, data, taps):
    segments, replicas = data.shape[0], data.shape[1]
    vmem = pl.BlockSpec(memory_space=pltpu.VMEM)
    return pl.pallas_call(
        transform_kernel,
        out_shape=(
            jax.ShapeDtypeStruct(data.shape, jnp.bfloat16),
            jax.ShapeDtypeStruct((segments, SUB + replicas, LANES), jnp.float32),
        ),
        in_specs=[vmem] * 8,
        out_specs=(vmem, vmem),
        compiler_params=pltpu.CompilerParams(vmem_limit_bytes=48 << 20),
        cost_estimate=pl.CostEstimate(flops=7_000_000_000, bytes_accessed=5_000_000, transcendentals=500_000),
    )(scales, data, taps, *[jnp.asarray(t) for t in tables()])


def to_peer(source, target, sems, row, seq, dp):
    return pltpu.make_async_remote_copy(
        src_ref=source, dst_ref=target, send_sem=sems.at[0, row], recv_sem=sems.at[1, row],
        device_id={"seq": seq, "dp": dp}, device_id_type=pl.DeviceIdType.MESH,
    )


def greet(seqs, dps, seq, dp):
    barrier = pltpu.get_barrier_semaphore()
    count = seqs * dps
    mine = seq * dps + dp

    def signal(offset, carry):
        peer = lax.rem(mine + offset, count)
        pl.semaphore_signal(
            barrier, inc=1, device_id={"seq": peer // dps, "dp": lax.rem(peer, dps)}, device_id_type=pl.DeviceIdType.MESH
        )
        return carry

    lax.fori_loop(1, count, signal, 0)
    pl.semaphore_wait(barrier, count - 1)


def send_all(seqs, dps, seq, dp, source_ref, target_ref, sems, row):
    count = seqs * dps
    mine = seq * dps + dp

    def send(offset, carry):
        peer = lax.rem(mine + offset * STRIDE, count)
        to_peer(source_ref.at[peer], target_ref.at[mine], sems, row, peer // dps, lax.rem(peer, dps)).start()
        return carry

    lax.fori_loop(1, count, send, 0)


def gather_kernel(seqs, dps, data_ref, taps_ref, scale_ref, got_ref, taps_got_ref, scales_got_ref,
                  dp_scale, scale_tile, sems, local_sems):
    seq, dp = lax.axis_index("seq"), lax.axis_index("dp")
    mine = seq * dps + dp
    greet(seqs, dps, seq, dp)

    def send_scale(offset, carry):
        to_peer(scale_ref, dp_scale.at[dp], sems, 0, seq, lax.rem(dp + offset, dps)).start()
        return carry

    lax.fori_loop(1, dps, send_scale, 0)
    send_all(seqs, dps, seq, dp, data_ref, got_ref, sems, 1)

    def send_taps(offset, carry):
        peer = lax.rem(seq + offset, seqs)
        to_peer(taps_ref.at[peer, dp], taps_got_ref.at[seq], sems, 2, peer, dp).start()
        return carry

    lax.fori_loop(1, seqs, send_taps, 0)
    own = pltpu.make_async_copy(data_ref.at[mine], got_ref.at[mine], local_sems.at[0])
    own.start()
    own_taps = pltpu.make_async_copy(taps_ref.at[seq, dp], taps_got_ref.at[seq], local_sems.at[1])
    own_taps.start()

    next_dp, next_seq = lax.rem(dp + 1, dps), lax.rem(seq + 1, seqs)
    to_peer(dp_scale.at[pl.ds(0, dps - 1)], dp_scale.at[pl.ds(0, dps - 1)], sems, 0, seq, next_dp).wait()
    own.wait()
    own_taps.wait()
    dp_scale[dp] = scale_ref[...]
    for other in range(dps):
        scale_tile[other : other + 1] = dp_scale[other, 0:1]

    def send_tile(offset, carry):
        to_peer(scale_tile, scales_got_ref.at[seq], sems, 3, lax.rem(seq + offset, seqs), dp).start()
        return carry

    lax.fori_loop(1, seqs, send_tile, 0)
    rest = pl.ds(0, seqs - 1)
    to_peer(taps_got_ref.at[rest], taps_got_ref.at[rest], sems, 2, next_seq, dp).wait()
    rest_all = pl.ds(0, seqs * dps - 1)
    to_peer(got_ref.at[rest_all], got_ref.at[rest_all], sems, 1, next_seq, dp).wait()
    to_peer(scales_got_ref.at[rest], scales_got_ref.at[rest], sems, 3, next_seq, dp).wait()
    scales_got_ref[seq] = scale_tile[...]


def gather(data, taps, scale):
    seqs, dps = taps.shape[0], taps.shape[1]
    vmem = pl.BlockSpec(memory_space=pltpu.VMEM)
    return pl.pallas_call(
        functools.partial(gather_kernel, seqs, dps),
        out_shape=(
            jax.ShapeDtypeStruct(data.shape, data.dtype),
            jax.ShapeDtypeStruct((seqs, SUB, LANES), jnp.float32),
            jax.ShapeDtypeStruct((seqs, SUB, LANES), jnp.float32),
        ),
        in_specs=[vmem] * 3,
        out_specs=(vmem,) * 3,
        scratch_shapes=[
            pltpu.VMEM((dps, SUB, LANES), jnp.float32),
            pltpu.VMEM((SUB, LANES), jnp.float32),
            pltpu.SemaphoreType.DMA((2, 4)),
            pltpu.SemaphoreType.DMA((2,)),
        ],
        compiler_params=pltpu.CompilerParams(collective_id=0, has_side_effects=True, vmem_limit_bytes=48 << 20),
    )(data, taps, scale)


def scatter_kernel(seqs, dps, data_ref, grad_ref, got_ref, grad_got_ref, scale_got_ref,
                   held, rows, sems, local_sems):
    seq, dp = lax.axis_index("seq"), lax.axis_index("dp")
    mine = seq * dps + dp
    pairs = dps // 2
    pair, parity = dp // 2, lax.rem(dp, 2)
    greet(seqs, dps, seq, dp)

    def send_grad(offset, carry):
        peer_seq = lax.rem(seq + offset // 2, seqs)
        peer_dp = pair * 2 + lax.rem(parity + offset, 2)
        to_peer(grad_ref.at[peer_seq], held.at[parity * seqs + seq], sems, 0, peer_seq, peer_dp).start()
        return carry

    lax.fori_loop(1, 2 * seqs, send_grad, 0)
    send_all(seqs, dps, seq, dp, data_ref, got_ref, sems, 1)
    own = pltpu.make_async_copy(data_ref.at[mine], got_ref.at[mine], local_sems.at[0])
    own.start()
    own_grad = pltpu.make_async_copy(grad_ref.at[seq], held.at[parity * seqs + seq], local_sems.at[1])
    own_grad.start()

    next_seq = lax.rem(seq + 1, seqs)
    rest = pl.ds(0, 2 * seqs - 1)
    to_peer(held.at[rest], held.at[rest], sems, 0, next_seq, dp).wait()
    own.wait()
    own_grad.wait()
    for other in range(pairs):
        rows[other] = held[:, SUB + other * 2 + parity]

    def send_along(offset, carry):
        peer = lax.rem(pair + offset, pairs)
        peer_dp = peer * 2 + parity
        to_peer(held.at[:, pl.ds(0, SUB)], grad_got_ref.at[pair], sems, 2, seq, peer_dp).start()
        to_peer(rows.at[peer], scale_got_ref.at[pair], sems, 3, seq, peer_dp).start()
        return carry

    lax.fori_loop(1, pairs, send_along, 0)
    own_held = pltpu.make_async_copy(held.at[:, pl.ds(0, SUB)], grad_got_ref.at[pair], local_sems.at[0])
    own_held.start()
    own_rows = pltpu.make_async_copy(rows.at[pair], scale_got_ref.at[pair], local_sems.at[1])
    own_rows.start()
    rest_pairs = pl.ds(0, pairs - 1)
    next_dp = lax.rem(dp + 2, dps)
    to_peer(grad_got_ref.at[rest_pairs], grad_got_ref.at[rest_pairs], sems, 2, seq, next_dp).wait()
    to_peer(scale_got_ref.at[rest_pairs], scale_got_ref.at[rest_pairs], sems, 3, seq, next_dp).wait()
    rest_all = pl.ds(0, seqs * dps - 1)
    to_peer(got_ref.at[rest_all], got_ref.at[rest_all], sems, 1, next_seq, dp).wait()
    own_held.wait()
    own_rows.wait()


def scatter(data, grad, dps):
    seqs = grad.shape[0]
    pairs = dps // 2
    vmem = pl.BlockSpec(memory_space=pltpu.VMEM)
    return pl.pallas_call(
        functools.partial(scatter_kernel, seqs, dps),
        out_shape=(
            jax.ShapeDtypeStruct(data.shape, data.dtype),
            jax.ShapeDtypeStruct((pairs, 2 * seqs, SUB, LANES), jnp.float32),
            jax.ShapeDtypeStruct((pairs, 2 * seqs, LANES), jnp.float32),
        ),
        in_specs=[vmem] * 2,
        out_specs=(vmem,) * 3,
        scratch_shapes=[
            pltpu.VMEM((2 * seqs, 2 * SUB, LANES), jnp.float32),
            pltpu.VMEM((pairs, 2 * seqs, LANES), jnp.float32),
            pltpu.SemaphoreType.DMA((2, 4)),
            pltpu.SemaphoreType.DMA((2,)),
        ],
        compiler_params=pltpu.CompilerParams(collective_id=1, has_side_effects=True, vmem_limit_bytes=48 << 20),
    )(data, grad)


def by_channel(value):
    return value.reshape(SUB, LANES, value.shape[-1]).transpose(2, 0, 1)


def by_position(value):
    return value.transpose(1, 2, 0).reshape(SUB * LANES, value.shape[0])


def on_device(activations, gate_values, output_grad, filter_codes, filter_scales):
    channels = filter_codes.shape[1]
    seqs, replicas = lax.axis_size("seq"), lax.axis_size("dp")
    block_size = filter_codes.shape[0] // filter_scales.shape[0]
    grad_in = output_grad[0].astype(jnp.float32)
    act = grad_in * gate_values[0].astype(jnp.float32)
    top = jnp.maximum(jnp.max(jnp.abs(act)), FLOOR)
    act_code = eighth_power(act * (TOP8 / top)).astype(jnp.bfloat16)
    sent = jnp.concatenate([by_channel(activations[0]), by_channel(act_code)], axis=1)
    scale_rows = jnp.repeat(filter_scales, block_size, axis=0)
    taps = by_channel(filter_codes.astype(jnp.float32) * scale_rows)
    got, taps_got, scales_got = gather(
        sent, taps.reshape(seqs, replicas, SUB, LANES), jnp.full((SUB, LANES), top * (1.0 / TOP8), jnp.float32)
    )
    out, grad = transforms(scales_got, got.reshape(seqs, replicas, 2 * SUB, LANES), taps_got.reshape(ROWS, LANES))
    back, grad_all, scale_all = scatter(out.reshape(channels, 2 * SUB, LANES), grad, replicas)
    grad_all = grad_all.reshape(replicas // 2, 2, seqs, SUB, LANES).transpose(2, 0, 1, 3, 4).reshape(channels, SUB, LANES)
    scale_all = scale_all.reshape(replicas // 2, 2, seqs, LANES).transpose(2, 0, 1, 3).reshape(channels, LANES)

    back = back.astype(jnp.float32)
    conv = by_position(root_of(back[:, :SUB], 4) * scale_all[:, 0, None, None])
    input_grad = by_position(root_of(back[:, SUB:], 3) * scale_all[:, LANES // 2, None, None])
    gate_grad = (grad_in * conv).astype(jnp.bfloat16)
    code_grad = by_position(grad_all) * scale_rows
    return (input_grad[None], gate_grad[None], code_grad)


def solution(mesh):
    in_specs = (
        P("dp", "seq", None),
        P("dp", "seq", None),
        P("dp", "seq", None),
        P("seq", None),
        P("seq", None),
    )
    out_specs = (P("dp", "seq", None), P("dp", "seq", None), P("seq", None))
    return jax.shard_map(on_device, mesh=mesh, in_specs=in_specs, out_specs=out_specs, check_vma=False)
```

```python
import functools

import jax
import jax.numpy as jnp
import numpy as np
from jax import lax
from jax.experimental import pallas as pl
from jax.experimental.pallas import tpu as pltpu
from jax.sharding import PartitionSpec as P

LANES = 128
SUB = 8
ROWS = 256
FLOOR = 2.0**-90
TOP8 = 2.0**15
TOP12 = 2.0**2.5
TOP8_RMS = 2.0**7.75
RMS_FLOOR = 2.0**-50


def split_np(table):
    high = np.asarray(table, np.float64).astype(jnp.bfloat16)
    low = (np.asarray(table, np.float64) - high.astype(np.float64)).astype(jnp.bfloat16)
    return high, low


def tables():
    whole = 2 * ROWS * LANES
    rows = np.arange(ROWS, dtype=np.float64)
    lanes = np.arange(LANES, dtype=np.float64)
    outer = 2 * np.pi * (rows[:, None] + 0.5) * rows[None, :] / (2 * ROWS)
    first = np.concatenate([np.cos(outer), -np.sin(outer)], axis=0)
    last = np.concatenate([np.cos(outer.T), -np.sin(outer.T)], axis=1) * (2.0 / whole)
    inner = 2 * np.pi * lanes[:, None] * lanes[None, :] / LANES
    cos, sin = np.cos(inner), np.sin(inner)
    forward = np.block([[cos, -sin], [sin, cos]])
    backward = np.block([[cos, sin], [-sin, cos]])
    turn = 2 * np.pi * (rows[:, None] + 0.5) * lanes[None, :] / whole
    twist = np.stack([np.cos(turn), -np.sin(turn)]).astype(np.float32)
    first_hi, first_lo = split_np(first)
    last_hi, last_lo = split_np(last)
    return (
        np.concatenate([first_hi, first_lo], axis=0),
        np.concatenate([last_hi, last_lo], axis=0),
        np.stack(split_np(forward)),
        np.stack(split_np(backward)),
        twist,
    )


def dot(left, right):
    return jnp.dot(left, right, preferred_element_type=jnp.float32)


def halves(value):
    high = value.astype(jnp.bfloat16)
    low = (value - high.astype(jnp.float32)).astype(jnp.bfloat16)
    return high, low


def left_product(table_ref, high, low):
    count = table_ref.shape[0] // 2
    both = dot(table_ref[...], high)
    total = both[:count] + both[count:]
    if low is not None:
        total = total + dot(table_ref[:count], low)
    return total


def right_product(value, table_ref):
    high, low = halves(value)
    return dot(high, table_ref[0]) + dot(low, table_ref[0]) + dot(high, table_ref[1])


def forward(high, low, first_ref, forward_ref, twist_ref):
    section = left_product(first_ref, high, low)
    cos, sin = twist_ref[0], twist_ref[1]
    out = []
    for start in range(0, high.shape[1], LANES):
        real = section[:ROWS, start : start + LANES]
        imag = section[ROWS:, start : start + LANES]
        turned = jnp.concatenate([real * cos - imag * sin, real * sin + imag * cos], axis=1)
        out.append(right_product(turned, forward_ref))
    return out


def inverse(spectra, last_ref, backward_ref, twist_ref):
    cos, sin = twist_ref[0], twist_ref[1]
    sections = []
    for spec in spectra:
        part = right_product(spec, backward_ref)
        real, imag = part[:, :LANES], part[:, LANES:]
        sections.append(jnp.concatenate([real * cos + imag * sin, imag * cos - real * sin], axis=0))
    high, low = halves(jnp.concatenate(sections, axis=1))
    result = left_product(last_ref, high, low)
    return [result[:, i * LANES : (i + 1) * LANES] for i in range(len(spectra))]


def times(left, right):
    lr, li, rr, ri = left[:, :LANES], left[:, LANES:], right[:, :LANES], right[:, LANES:]
    return jnp.concatenate([lr * rr - li * ri, lr * ri + li * rr], axis=1)


def times_conj(left, right):
    lr, li, rr, ri = left[:, :LANES], left[:, LANES:], right[:, :LANES], right[:, LANES:]
    return jnp.concatenate([lr * rr + li * ri, li * rr - lr * ri], axis=1)


def eighth_power(value):
    two = value * value
    four = two * two
    return four * two * value * jnp.abs(value)


def twelfth_power(value):
    two = value * value
    four = two * two
    return four * four * two * value * jnp.abs(value)


def root_of(code, power):
    size = jnp.exp2(jnp.log2(jnp.abs(code)) * (1.0 / power))
    return jnp.where(code < 0, -size, size)


def root_mean_square(spec):
    whole = 2 * ROWS * LANES
    return jnp.sqrt(jnp.sum(spec * spec, keepdims=True) * (2.0 / whole)) * (1.0 / whole) ** 0.5


def to_peer(source, target, send_sem, recv_sem, seq, dp):
    return pltpu.make_async_remote_copy(
        src_ref=source, dst_ref=target, send_sem=send_sem, recv_sem=recv_sem,
        device_id={"seq": seq, "dp": dp}, device_id_type=pl.DeviceIdType.MESH,
    )


def greet(seqs, dps, seq, dp, ready):
    barrier = pltpu.get_barrier_semaphore()
    chips = seqs // 2
    core, chip = lax.rem(seq, 2), seq // 2
    near = 2 * dps

    def tell(sem, seq_to, dp_to):
        pl.semaphore_signal(sem, inc=1, device_id={"seq": seq_to, "dp": dp_to}, device_id_type=pl.DeviceIdType.MESH)

    def tell_near(offset, carry):
        peer = lax.rem(core * dps + dp + offset, near)
        tell(barrier, chip * 2 + peer // dps, lax.rem(peer, dps))
        return carry

    def tell_far(sem):
        def body(offset, carry):
            tell(sem, lax.rem(chip + offset, chips) * 2 + core, dp)
            return carry

        return body

    lax.fori_loop(1, chips, tell_far(barrier), 0)
    lax.fori_loop(1, near, tell_near, 0)
    pl.semaphore_wait(barrier, near + chips - 2)
    lax.fori_loop(1, chips, tell_far(ready), 0)
    pl.semaphore_wait(ready, chips - 1)


SCALE, TAPS, SCALES, GRAD, RMS, BACK, GRAD_Y, RMS_Y, DATA = range(9)


def main_kernel(
    seqs, dps, data_ref, taps_ref, scale_ref, first_ref, last_ref, forward_ref, backward_ref, twist_ref,
    back_ref, grad_all_ref, rms_all_ref,
    got, taps_got, scale_got, scale_row, scales_got, conv_specs, back_specs, cross_ref, out, grad, rms, held, held_rms,
    send_sems, recv_sems, local_sems, ready,
):
    seq, dp = lax.axis_index("seq"), lax.axis_index("dp")
    mine = seq * dps + dp
    pairs = dps // 2
    pair, parity = dp // 2, lax.rem(dp, 2)
    next_seq = lax.rem(seq + 1, seqs)
    lane = lax.broadcasted_iota(jnp.int32, (1, LANES), 1)
    group = LANES // dps
    half_group = group // 2

    def copy_to(source, target, kind, seq_to, dp_to, recv_kind=None):
        return to_peer(
            source, target, send_sems.at[kind], recv_sems.at[kind if recv_kind is None else recv_kind], seq_to, dp_to
        )

    def of(ref, count, kind, recv_kind=None):
        part = ref.at[pl.ds(0, count)]
        return copy_to(part, part, kind, next_seq, dp, recv_kind)

    greet(seqs, dps, seq, dp, ready)

    def send_scale(offset, carry):
        copy_to(scale_ref, scale_got.at[dp], SCALE, seq, lax.rem(dp + offset, dps)).start()
        return carry

    lax.fori_loop(1, dps, send_scale, 0)

    def send_taps(offset, carry):
        peer = lax.rem(seq + offset, seqs)
        copy_to(taps_ref.at[peer, dp], taps_got.at[seq], TAPS, peer, dp).start()
        return carry

    lax.fori_loop(1, seqs, send_taps, 0)

    def send_pair(step, source_of, target, kind, recv_kind):
        peer_pair = lax.rem(pair + step, pairs)

        def send(offset, carry):
            peer_seq = lax.rem(seq + offset // 2, seqs)
            peer_dp = peer_pair * 2 + lax.rem(parity + offset, 2)
            copy_to(source_of(peer_seq, peer_dp), target.at[mine], kind, peer_seq, peer_dp, recv_kind).start()
            return carry

        lax.fori_loop(jnp.where(step == 0, 1, 0), 2 * seqs, send, 0)

    def send_data(step, carry):
        send_pair(step, lambda s, d: data_ref.at[s * dps + d], got, DATA, DATA + pair)
        return carry

    lax.fori_loop(0, pairs, send_data, 0)
    own = pltpu.make_async_copy(data_ref.at[mine], got.at[mine], local_sems.at[0])
    own.start()
    own_taps = pltpu.make_async_copy(taps_ref.at[seq, dp], taps_got.at[seq], local_sems.at[1])
    own_taps.start()

    of(scale_got, dps - 1, SCALE).wait()
    scale_got[dp] = scale_ref[...]
    row = jnp.zeros((1, LANES), jnp.float32)
    for other in range(dps):
        row = jnp.where(lane // group == other, scale_got[other], row)
    scale_row[...] = row

    def send_row(offset, carry):
        copy_to(scale_row, scales_got.at[seq], SCALES, lax.rem(seq + offset, seqs), dp).start()
        return carry

    lax.fori_loop(1, seqs, send_row, 0)

    own_taps.wait()
    of(taps_got, seqs - 1, TAPS).wait()
    taps_high, taps_low = halves(taps_got[...].reshape(ROWS, LANES))
    (taps_spec,) = forward(taps_high, taps_low, first_ref, forward_ref, twist_ref)
    cross_ref[...] = jnp.zeros_like(cross_ref)
    own.wait()
    of(scales_got, seqs - 1, SCALES).wait()
    scales_got[seq] = scale_row[...]
    of(got, 2 * seqs - 1, DATA, DATA + pair).wait_recv()
    rms[...] = jnp.zeros_like(rms)

    def transform_pair(step, carry):
        source = lax.rem(pair + pairs - step, pairs)

        @pl.when(step > 0)
        def _():
            of(got, 2 * seqs, DATA, DATA + source).wait_recv()

        signals, acts = [], []
        for half in range(2):
            index = source * 2 + half
            tile = jnp.stack([got[s * dps + index] for s in range(seqs)]).astype(jnp.float32)
            signals.append(tile[:, :SUB].reshape(ROWS, LANES).astype(jnp.bfloat16))
            scale = jnp.max(jnp.where(lane // group == index, scales_got[...], 0.0), axis=-1, keepdims=True)
            acts.append((root_of(tile[:, SUB:], 8) * scale).reshape(ROWS, LANES))
        act_high, act_low = halves(jnp.concatenate(acts, axis=1))
        signal_specs = forward(jnp.concatenate(signals, axis=1), None, first_ref, forward_ref, twist_ref)
        act_specs = forward(act_high, act_low, first_ref, forward_ref, twist_ref)
        for half, (signal_spec, act_spec) in enumerate(zip(signal_specs, act_specs)):
            index = source * 2 + half
            cross_ref[...] += times_conj(act_spec, signal_spec)
            conv_spec, back_spec = times(signal_spec, carry), times_conj(act_spec, carry)
            conv_specs[index] = conv_spec
            back_specs[index] = back_spec
            conv_rms = jnp.maximum(root_mean_square(conv_spec), RMS_FLOOR)
            back_rms = jnp.maximum(root_mean_square(back_spec), RMS_FLOOR)
            both = jnp.where(lane % group < half_group, conv_rms, back_rms)
            rms[...] = jnp.where(lane // group == index, both, rms[...])
        return carry

    taps_spec = lax.fori_loop(0, pairs, transform_pair, taps_spec)

    (grad_value,) = inverse([cross_ref[...]], last_ref, backward_ref, twist_ref)
    grad[...] = grad_value.reshape(seqs, SUB, LANES)

    def send_grad(offset, carry):
        peer_seq = lax.rem(seq + offset // 2, seqs)
        peer_dp = pair * 2 + lax.rem(parity + offset, 2)
        copy_to(grad.at[peer_seq], held.at[parity * seqs + seq], GRAD, peer_seq, peer_dp).start()
        copy_to(rms, held_rms.at[parity * seqs + seq], RMS, peer_seq, peer_dp).start()
        return carry

    lax.fori_loop(1, 2 * seqs, send_grad, 0)

    def invert_pair(step, carry):
        target = lax.rem(pair + step, pairs)
        convs = inverse([conv_specs[target * 2], conv_specs[target * 2 + 1]], last_ref, backward_ref, twist_ref)
        backs = inverse([back_specs[target * 2], back_specs[target * 2 + 1]], last_ref, backward_ref, twist_ref)
        for half in range(2):
            index = target * 2 + half
            here = (lane // group == index) & (lane % half_group == 0)
            both = jnp.where(here, rms[...], 0.0)
            conv_rms = jnp.sum(jnp.where(lane % group < half_group, both, 0.0), keepdims=True)
            back_rms = jnp.sum(jnp.where(lane % group < half_group, 0.0, both), keepdims=True)
            conv_code = twelfth_power(convs[half] * (TOP12 / conv_rms)).reshape(seqs, SUB, LANES)
            back_code = eighth_power(backs[half] * (TOP8_RMS / back_rms)).reshape(seqs, SUB, LANES)
            out[index] = jnp.concatenate([conv_code, back_code], axis=1).astype(jnp.bfloat16)
        send_pair(step, lambda s, d: out.at[d, s], back_ref, BACK, BACK)
        return carry

    lax.fori_loop(0, pairs, invert_pair, 0)
    own_back = pltpu.make_async_copy(out.at[dp, seq], back_ref.at[mine], local_sems.at[0])
    own_back.start()

    of(held, 2 * seqs - 1, GRAD).wait()
    of(held_rms, 2 * seqs - 1, RMS).wait()
    held[parity * seqs + seq] = grad[seq]
    held_rms[parity * seqs + seq] = rms[...]

    def send_along(offset, carry):
        peer_dp = lax.rem(pair + offset, pairs) * 2 + parity
        copy_to(held, grad_all_ref.at[pair], GRAD_Y, seq, peer_dp).start()
        copy_to(held_rms, rms_all_ref.at[pair], RMS_Y, seq, peer_dp).start()
        return carry

    lax.fori_loop(1, pairs, send_along, 0)
    own_held = pltpu.make_async_copy(held, grad_all_ref.at[pair], local_sems.at[1])
    own_held.start()
    own_rms = pltpu.make_async_copy(held_rms, rms_all_ref.at[pair], local_sems.at[2])
    own_rms.start()
    own_back.wait()
    own_held.wait()
    own_rms.wait()
    of(got, seqs * dps - 1, DATA).wait_send()
    of(grad_all_ref, pairs - 1, GRAD_Y).wait()
    of(rms_all_ref, pairs - 1, RMS_Y).wait()
    of(back_ref, seqs * dps - 1, BACK).wait()


def exchange(data, taps, scale):
    seqs, dps = taps.shape[0], taps.shape[1]
    pairs = dps // 2
    vmem = pl.BlockSpec(memory_space=pltpu.VMEM)
    f32, bf16 = jnp.float32, jnp.bfloat16
    return pl.pallas_call(
        functools.partial(main_kernel, seqs, dps),
        out_shape=(
            jax.ShapeDtypeStruct(data.shape, bf16),
            jax.ShapeDtypeStruct((pairs, 2 * seqs, SUB, LANES), f32),
            jax.ShapeDtypeStruct((pairs, 2 * seqs, 1, LANES), f32),
        ),
        in_specs=[vmem] * 8,
        out_specs=(vmem,) * 3,
        scratch_shapes=[
            pltpu.VMEM(data.shape, bf16),
            pltpu.VMEM((seqs, SUB, LANES), f32),
            pltpu.VMEM((dps, 1, LANES), f32),
            pltpu.VMEM((1, LANES), f32),
            pltpu.VMEM((seqs, 1, LANES), f32),
            pltpu.VMEM((dps, ROWS, 2 * LANES), f32),
            pltpu.VMEM((dps, ROWS, 2 * LANES), f32),
            pltpu.VMEM((ROWS, 2 * LANES), f32),
            pltpu.VMEM((dps, seqs, 2 * SUB, LANES), bf16),
            pltpu.VMEM((seqs, SUB, LANES), f32),
            pltpu.VMEM((1, LANES), f32),
            pltpu.VMEM((2 * seqs, SUB, LANES), f32),
            pltpu.VMEM((2 * seqs, 1, LANES), f32),
            pltpu.SemaphoreType.DMA((DATA + 1,)),
            pltpu.SemaphoreType.DMA((DATA + pairs,)),
            pltpu.SemaphoreType.DMA((3,)),
            pltpu.SemaphoreType.REGULAR,
        ],
        compiler_params=pltpu.CompilerParams(collective_id=0, has_side_effects=True, vmem_limit_bytes=48 << 20),
    )(data, taps, scale, *[jnp.asarray(t) for t in tables()])


def by_channel(value):
    return value.reshape(SUB, LANES, value.shape[-1]).transpose(2, 0, 1)


def by_position(value):
    return value.transpose(1, 2, 0).reshape(SUB * LANES, value.shape[0])


def on_device(activations, gate_values, output_grad, filter_codes, filter_scales):
    channels = filter_codes.shape[1]
    seqs, replicas = lax.axis_size("seq"), lax.axis_size("dp")
    block_size = filter_codes.shape[0] // filter_scales.shape[0]
    grad_in = output_grad[0].astype(jnp.float32)
    act = grad_in * gate_values[0].astype(jnp.float32)
    top = jnp.maximum(jnp.max(jnp.abs(act)), FLOOR)
    act_code = eighth_power(act * (TOP8 / top)).astype(jnp.bfloat16)
    sent = jnp.concatenate([by_channel(activations[0]), by_channel(act_code)], axis=1)
    scale_rows = jnp.repeat(filter_scales, block_size, axis=0)
    taps = by_channel(filter_codes.astype(jnp.float32) * scale_rows)
    back, grad_all, rms_all = exchange(
        sent, taps.reshape(seqs, replicas, SUB, LANES), jnp.full((1, LANES), top * (1.0 / TOP8), jnp.float32)
    )
    grad_all = grad_all.reshape(replicas // 2, 2, seqs, SUB, LANES).transpose(2, 0, 1, 3, 4).reshape(channels, SUB, LANES)
    rms_all = rms_all.reshape(replicas // 2, 2, seqs, LANES).transpose(2, 0, 1, 3).reshape(channels, replicas, 2, -1)
    rms_all = lax.dynamic_index_in_dim(rms_all[..., 0], lax.axis_index("dp"), 1, keepdims=False)

    back = back.astype(jnp.float32)
    conv = by_position(root_of(back[:, :SUB], 12) * (rms_all[:, 0] * (1.0 / TOP12))[:, None, None])
    input_grad = by_position(root_of(back[:, SUB:], 8) * (rms_all[:, 1] * (1.0 / TOP8_RMS))[:, None, None])
    gate_grad = (grad_in * conv).astype(jnp.bfloat16)
    code_grad = by_position(grad_all) * scale_rows
    return (input_grad[None], gate_grad[None], code_grad)


def solution(mesh):
    in_specs = (
        P("dp", "seq", None),
        P("dp", "seq", None),
        P("dp", "seq", None),
        P("seq", None),
        P("seq", None),
    )
    out_specs = (P("dp", "seq", None), P("dp", "seq", None), P("seq", None))
    return jax.shard_map(on_device, mesh=mesh, in_specs=in_specs, out_specs=out_specs, check_vma=False)
```

```python
import functools

import jax
import jax.numpy as jnp
import numpy as np
from jax import lax
from jax.experimental import pallas as pl
from jax.experimental.pallas import tpu as pltpu
from jax.sharding import PartitionSpec as P

LANES = 128
SUB = 8
ROWS = 256
FLOOR = 2.0**-90
TOP8 = 2.0**15
TOP14 = 2.0
TOP8_RMS = 2.0**7.75
RMS_FLOOR = 2.0**-50


def split_np(table):
    high = np.asarray(table, np.float64).astype(jnp.bfloat16)
    low = (np.asarray(table, np.float64) - high.astype(np.float64)).astype(jnp.bfloat16)
    return high, low


def tables():
    whole = 2 * ROWS * LANES
    rows = np.arange(ROWS, dtype=np.float64)
    lanes = np.arange(LANES, dtype=np.float64)
    outer = 2 * np.pi * (rows[:, None] + 0.5) * rows[None, :] / (2 * ROWS)
    first = np.concatenate([np.cos(outer), -np.sin(outer)], axis=0)
    last = np.concatenate([np.cos(outer.T), -np.sin(outer.T)], axis=1) * (2.0 / whole)
    inner = 2 * np.pi * lanes[:, None] * lanes[None, :] / LANES
    cos, sin = np.cos(inner), np.sin(inner)
    forward = np.block([[cos, -sin], [sin, cos]])
    backward = np.block([[cos, sin], [-sin, cos]])
    turn = 2 * np.pi * (rows[:, None] + 0.5) * lanes[None, :] / whole
    twist = np.stack([np.cos(turn), -np.sin(turn)]).astype(np.float32)
    first_hi, first_lo = split_np(first)
    last_hi, last_lo = split_np(last)
    return (
        np.concatenate([first_hi, first_lo], axis=0),
        np.concatenate([last_hi, last_lo], axis=0),
        np.stack(split_np(forward)),
        np.stack(split_np(backward)),
        twist,
    )


def dot(left, right):
    return jnp.dot(left, right, preferred_element_type=jnp.float32)


def halves(value):
    high = value.astype(jnp.bfloat16)
    low = (value - high.astype(jnp.float32)).astype(jnp.bfloat16)
    return high, low


def left_product(table_ref, high, low):
    count = table_ref.shape[0] // 2
    both = dot(table_ref[...], high)
    total = both[:count] + both[count:]
    if low is not None:
        total = total + dot(table_ref[:count], low)
    return total


def right_product(value, table_ref):
    high, low = halves(value)
    return dot(high, table_ref[0]) + dot(low, table_ref[0]) + dot(high, table_ref[1])


def forward(high, low, first_ref, forward_ref, twist_ref):
    section = left_product(first_ref, high, low)
    cos, sin = twist_ref[0], twist_ref[1]
    out = []
    for start in range(0, high.shape[1], LANES):
        real = section[:ROWS, start : start + LANES]
        imag = section[ROWS:, start : start + LANES]
        turned = jnp.concatenate([real * cos - imag * sin, real * sin + imag * cos], axis=1)
        out.append(right_product(turned, forward_ref))
    return out


def inverse(spectra, last_ref, backward_ref, twist_ref):
    cos, sin = twist_ref[0], twist_ref[1]
    sections = []
    for spec in spectra:
        part = right_product(spec, backward_ref)
        real, imag = part[:, :LANES], part[:, LANES:]
        sections.append(jnp.concatenate([real * cos + imag * sin, imag * cos - real * sin], axis=0))
    high, low = halves(jnp.concatenate(sections, axis=1))
    result = left_product(last_ref, high, low)
    return [result[:, i * LANES : (i + 1) * LANES] for i in range(len(spectra))]


def times(left, right):
    lr, li, rr, ri = left[:, :LANES], left[:, LANES:], right[:, :LANES], right[:, LANES:]
    return jnp.concatenate([lr * rr - li * ri, lr * ri + li * rr], axis=1)


def times_conj(left, right):
    lr, li, rr, ri = left[:, :LANES], left[:, LANES:], right[:, :LANES], right[:, LANES:]
    return jnp.concatenate([lr * rr + li * ri, li * rr - lr * ri], axis=1)


def eighth_power(value):
    two = value * value
    four = two * two
    return four * two * value * jnp.abs(value)


def fourteenth_power(value):
    two = value * value
    four = two * two
    return four * four * four * value * jnp.abs(value)


def root_of(code, power):
    size = jnp.exp2(jnp.log2(jnp.abs(code)) * (1.0 / power))
    return jnp.where(code < 0, -size, size)


def root_mean_square(spec):
    whole = 2 * ROWS * LANES
    return jnp.sqrt(jnp.sum(spec * spec, keepdims=True) * (2.0 / whole)) * (1.0 / whole) ** 0.5


def to_peer(source, target, send_sem, recv_sem, seq, dp):
    return pltpu.make_async_remote_copy(
        src_ref=source, dst_ref=target, send_sem=send_sem, recv_sem=recv_sem,
        device_id={"seq": seq, "dp": dp}, device_id_type=pl.DeviceIdType.MESH,
    )


def greet(seqs, dps, seq, dp, ready, meanwhile):
    barrier = pltpu.get_barrier_semaphore()
    chips = seqs // 2
    core, chip = lax.rem(seq, 2), seq // 2
    near = 2 * dps

    def tell(sem, seq_to, dp_to):
        pl.semaphore_signal(sem, inc=1, device_id={"seq": seq_to, "dp": dp_to}, device_id_type=pl.DeviceIdType.MESH)

    def tell_near(offset, carry):
        peer = lax.rem(core * dps + dp + offset, near)
        tell(barrier, chip * 2 + peer // dps, lax.rem(peer, dps))
        return carry

    def tell_far(sem):
        def body(offset, carry):
            tell(sem, lax.rem(chip + offset, chips) * 2 + core, dp)
            return carry

        return body

    lax.fori_loop(1, chips, tell_far(barrier), 0)
    lax.fori_loop(1, near, tell_near, 0)
    meanwhile()
    pl.semaphore_wait(barrier, near + chips - 2)
    lax.fori_loop(1, chips, tell_far(ready), 0)
    pl.semaphore_wait(ready, chips - 1)


SCALE, TAPS, SCALES, GRAD, RMS, BACK, GRAD_Y, RMS_Y, DATA = range(9)
CONV_LANE, GRAD_LANE, BACK_LANE = 0, 4, 8


def lane_of(rows, lane, wanted):
    return jnp.max(jnp.where(lane == wanted, rows, 0.0), axis=-1, keepdims=True)


def main_kernel(
    seqs, dps, acts_hbm, gate_hbm, cot_hbm, codes_hbm, filter_scale_ref,
    first_hbm, last_hbm, forward_hbm, backward_hbm, twist_hbm,
    back_ref, grad_all_ref, rms_all_ref,
    acts_ref, gate_ref, cot_ref, codes_ref, first_ref, last_ref, forward_ref, backward_ref, twist_ref,
    turned, taps_ref, data_ref, scale_ref,
    got, taps_got, scale_got, scale_row, scales_got, conv_specs, back_specs, cross_ref, out, grad, rms, held, held_rms,
    grad_code, send_sems, recv_sems, local_sems, load_sems, ready,
):
    seq, dp = lax.axis_index("seq"), lax.axis_index("dp")
    mine = dp * seqs + seq
    pairs = dps // 2
    pair, parity = dp // 2, lax.rem(dp, 2)
    next_seq = lax.rem(seq + 1, seqs)
    lane = lax.broadcasted_iota(jnp.int32, (1, LANES), 1)
    group = LANES // dps
    channels = seqs * dps

    loads = [
        pltpu.make_async_copy(source, target, load_sems.at[i])
        for i, (source, target) in enumerate(
            [(cot_hbm, cot_ref), (gate_hbm, gate_ref), (acts_hbm, acts_ref), (codes_hbm, codes_ref),
             (twist_hbm, twist_ref), (first_hbm, first_ref), (forward_hbm, forward_ref),
             (backward_hbm, backward_ref), (last_hbm, last_ref)]
        )
    ]
    for load in loads:
        load.start()

    def turn():
        for load in loads[:4]:
            load.wait()

        def chunk(i, top):
            at = pl.ds(pl.multiple_of(i * LANES, LANES), LANES)
            acts = acts_ref[at].astype(jnp.float32)
            grads = cot_ref[at].astype(jnp.float32) * gate_ref[at].astype(jnp.float32)
            taps = codes_ref[at].astype(jnp.float32) * filter_scale_ref[pl.ds(i, 1)]
            for start in range(0, channels, LANES):
                part = slice(start, start + LANES)
                turned[pl.ds(start * 2 * SUB + i, LANES, stride=2 * SUB)] = acts[:, part].T
                turned[pl.ds(start * 2 * SUB + SUB + i, LANES, stride=2 * SUB)] = grads[:, part].T
                taps_ref[pl.ds(start * SUB + i, LANES, stride=SUB)] = taps[:, part].T
            return jnp.maximum(top, jnp.max(jnp.abs(grads), axis=0, keepdims=True))

        top = lax.fori_loop(0, SUB, chunk, jnp.zeros((1, channels), jnp.float32))
        top = jnp.maximum(jnp.max(top, keepdims=True), FLOOR)
        scale_ref[...] = jnp.broadcast_to(top * (1.0 / TOP8), (1, LANES))
        factor = (TOP8 / top).reshape(1, 1, 1)

        def code(i, carry):
            tile = turned[pl.ds(pl.multiple_of(i * seqs * 2 * SUB, 2 * SUB), seqs * 2 * SUB)]
            tile = tile.reshape(seqs, 2 * SUB, LANES)
            coded = jnp.concatenate([tile[:, :SUB], eighth_power(tile[:, SUB:] * factor)], axis=1)
            data_ref[pl.ds(i * seqs, seqs)] = coded.astype(jnp.bfloat16)
            return carry

        lax.fori_loop(0, dps, code, 0)

    def copy_to(source, target, kind, seq_to, dp_to, recv_kind=None):
        return to_peer(
            source, target, send_sems.at[kind], recv_sems.at[kind if recv_kind is None else recv_kind], seq_to, dp_to
        )

    def of(ref, count, kind, recv_kind=None):
        part = ref.at[pl.ds(0, count)]
        return copy_to(part, part, kind, next_seq, dp, recv_kind)

    def taps_of(seq_to):
        return taps_ref.at[pl.ds(pl.multiple_of((dp * seqs + seq_to) * SUB, SUB), SUB)]

    greet(seqs, dps, seq, dp, ready, turn)

    def send_scale(offset, carry):
        copy_to(scale_ref, scale_got.at[dp], SCALE, seq, lax.rem(dp + offset, dps)).start()
        return carry

    lax.fori_loop(1, dps, send_scale, 0)

    def send_taps(offset, carry):
        peer = lax.rem(seq + offset, seqs)
        copy_to(taps_of(peer), taps_got.at[seq], TAPS, peer, dp).start()
        return carry

    lax.fori_loop(1, seqs, send_taps, 0)

    def send_pair(step, source_of, target, kind, recv_kind):
        peer_pair = lax.rem(pair + step, pairs)

        def send(offset, carry):
            peer_seq = lax.rem(seq + offset // 2, seqs)
            peer_dp = peer_pair * 2 + lax.rem(parity + offset, 2)
            copy_to(source_of(peer_seq, peer_dp), target.at[mine], kind, peer_seq, peer_dp, recv_kind).start()
            return carry

        lax.fori_loop(jnp.where(step == 0, 1, 0), 2 * seqs, send, 0)

    def send_data(step, carry):
        send_pair(step, lambda s, d: data_ref.at[d * seqs + s], got, DATA, DATA + pair)
        return carry

    lax.fori_loop(0, pairs, send_data, 0)
    own = pltpu.make_async_copy(data_ref.at[mine], got.at[mine], local_sems.at[0])
    own.start()
    own_taps = pltpu.make_async_copy(taps_of(seq), taps_got.at[seq], local_sems.at[1])
    own_taps.start()

    of(scale_got, dps - 1, SCALE).wait()
    scale_got[dp] = scale_ref[...]
    row = jnp.zeros((1, LANES), jnp.float32)
    for other in range(dps):
        row = jnp.where(lane // group == other, scale_got[other], row)
    scale_row[...] = row

    def send_row(offset, carry):
        copy_to(scale_row, scales_got.at[seq], SCALES, lax.rem(seq + offset, seqs), dp).start()
        return carry

    lax.fori_loop(1, seqs, send_row, 0)

    for load in loads[4:]:
        load.wait()
    own_taps.wait()
    of(taps_got, seqs - 1, TAPS).wait()
    taps_high, taps_low = halves(taps_got[...].reshape(ROWS, LANES))
    (taps_spec,) = forward(taps_high, taps_low, first_ref, forward_ref, twist_ref)
    cross_ref[...] = jnp.zeros_like(cross_ref)
    own.wait()
    of(scales_got, seqs - 1, SCALES).wait()
    scales_got[seq] = scale_row[...]
    of(got, 2 * seqs - 1, DATA, DATA + pair).wait_recv()
    rms[...] = jnp.zeros_like(rms)

    def transform_pair(step, carry):
        source = lax.rem(pair + pairs - step, pairs)

        @pl.when(step > 0)
        def _():
            of(got, 2 * seqs, DATA, DATA + source).wait_recv()

        signals, acts = [], []
        for half in range(2):
            index = source * 2 + half
            tile = got[pl.ds(index * seqs, seqs)].astype(jnp.float32)
            signals.append(tile[:, :SUB].reshape(ROWS, LANES).astype(jnp.bfloat16))
            scale = lane_of(scales_got[...], lane, index * group)
            acts.append((root_of(tile[:, SUB:], 8) * scale).reshape(ROWS, LANES))
        act_high, act_low = halves(jnp.concatenate(acts, axis=1))
        signal_specs = forward(jnp.concatenate(signals, axis=1), None, first_ref, forward_ref, twist_ref)
        act_specs = forward(act_high, act_low, first_ref, forward_ref, twist_ref)
        for half, (signal_spec, act_spec) in enumerate(zip(signal_specs, act_specs)):
            index = source * 2 + half
            cross_ref[...] += times_conj(act_spec, signal_spec)
            conv_spec, back_spec = times(signal_spec, carry), times_conj(act_spec, carry)
            conv_specs[index] = conv_spec
            back_specs[index] = back_spec
            conv_rms = jnp.maximum(root_mean_square(conv_spec), RMS_FLOOR)
            back_rms = jnp.maximum(root_mean_square(back_spec), RMS_FLOOR)
            both = jnp.where(lane % group < BACK_LANE, conv_rms, back_rms)
            rms[...] = jnp.where(lane // group == index, both, rms[...])
        return carry

    lax.fori_loop(0, pairs, transform_pair, taps_spec)

    cross = cross_ref[...]
    grad_rms = jnp.maximum(root_mean_square(cross), RMS_FLOOR)
    in_group = lane % group
    rms[...] = jnp.where((in_group >= GRAD_LANE) & (in_group < BACK_LANE), grad_rms, rms[...])
    (grad_value,) = inverse([cross], last_ref, backward_ref, twist_ref)
    grad[...] = grad_value.reshape(seqs, SUB, LANES)

    def send_grad(offset, carry):
        peer_seq = lax.rem(seq + offset // 2, seqs)
        peer_dp = pair * 2 + lax.rem(parity + offset, 2)
        copy_to(grad.at[peer_seq], held.at[parity * seqs + seq], GRAD, peer_seq, peer_dp).start()
        copy_to(rms, held_rms.at[parity * seqs + seq], RMS, peer_seq, peer_dp).start()
        return carry

    lax.fori_loop(1, 2 * seqs, send_grad, 0)

    def send_along_y():
        of(held, 2 * seqs - 1, GRAD).wait()
        of(held_rms, 2 * seqs - 1, RMS).wait()
        held[parity * seqs + seq] = grad[seq]
        held_rms[parity * seqs + seq] = rms[...]
        code = eighth_power(held[...] * (TOP8_RMS / lane_of(held_rms[...], lane, GRAD_LANE)))
        grad_code[...] = code.reshape(seqs, 2 * SUB, LANES).astype(jnp.bfloat16)

        def send_along(offset, carry):
            peer_dp = lax.rem(pair + offset, pairs) * 2 + parity
            copy_to(grad_code, grad_all_ref.at[pair], GRAD_Y, seq, peer_dp).start()
            copy_to(held_rms, rms_all_ref.at[pair], RMS_Y, seq, peer_dp).start()
            return carry

        lax.fori_loop(1, pairs, send_along, 0)

    def invert_pair(step, carry):
        target = lax.rem(pair + step, pairs)
        convs = inverse([conv_specs[target * 2], conv_specs[target * 2 + 1]], last_ref, backward_ref, twist_ref)
        backs = inverse([back_specs[target * 2], back_specs[target * 2 + 1]], last_ref, backward_ref, twist_ref)
        for half in range(2):
            index = target * 2 + half
            conv_rms = lane_of(rms[...], lane, index * group + CONV_LANE)
            back_rms = lane_of(rms[...], lane, index * group + BACK_LANE)
            conv_code = fourteenth_power(convs[half] * (TOP14 / conv_rms)).reshape(seqs, SUB, LANES)
            back_code = eighth_power(backs[half] * (TOP8_RMS / back_rms)).reshape(seqs, SUB, LANES)
            out[index] = jnp.concatenate([conv_code, back_code], axis=1).astype(jnp.bfloat16)

        @pl.when(step == 1)
        def _():
            send_along_y()

        send_pair(step, lambda s, d: out.at[d, s], back_ref, BACK, BACK)
        return carry

    lax.fori_loop(0, pairs, invert_pair, 0)
    own_back = pltpu.make_async_copy(out.at[dp, seq], back_ref.at[mine], local_sems.at[0])
    own_back.start()
    own_grad = pltpu.make_async_copy(grad_code, grad_all_ref.at[pair], local_sems.at[1])
    own_grad.start()
    own_rms = pltpu.make_async_copy(held_rms, rms_all_ref.at[pair], local_sems.at[2])
    own_rms.start()
    own_back.wait()
    own_grad.wait()
    own_rms.wait()
    of(got, channels - 1, DATA).wait_send()
    of(grad_all_ref, pairs - 1, GRAD_Y).wait()
    of(rms_all_ref, pairs - 1, RMS_Y).wait()
    of(back_ref, channels - 1, BACK).wait()


def exchange(seqs, dps, acts, gate, cot, codes, filter_scales):
    pairs, channels = dps // 2, seqs * dps
    vmem, hbm = pl.BlockSpec(memory_space=pltpu.VMEM), pl.BlockSpec(memory_space=pl.ANY)
    f32, bf16 = jnp.float32, jnp.bfloat16
    constants = [jnp.asarray(t) for t in tables()]
    first, last, forward_table, backward_table, twist = constants
    return pl.pallas_call(
        functools.partial(main_kernel, seqs, dps),
        out_shape=(
            jax.ShapeDtypeStruct((channels, 2 * SUB, LANES), bf16),
            jax.ShapeDtypeStruct((pairs, seqs, 2 * SUB, LANES), bf16),
            jax.ShapeDtypeStruct((pairs, 2 * seqs, 1, LANES), f32),
        ),
        in_specs=[hbm] * 4 + [vmem] + [hbm] * 5,
        out_specs=(vmem,) * 3,
        scratch_shapes=[pltpu.VMEM(value.shape, bf16) for value in (acts, gate, cot, codes)]
        + [pltpu.VMEM(value.shape, value.dtype) for value in constants]
        + [
            pltpu.VMEM((channels * 2 * SUB, LANES), f32),
            pltpu.VMEM((channels * SUB, LANES), f32),
            pltpu.VMEM((channels, 2 * SUB, LANES), bf16),
            pltpu.VMEM((1, LANES), f32),
            pltpu.VMEM((channels, 2 * SUB, LANES), bf16),
            pltpu.VMEM((seqs, SUB, LANES), f32),
            pltpu.VMEM((dps, 1, LANES), f32),
            pltpu.VMEM((1, LANES), f32),
            pltpu.VMEM((seqs, 1, LANES), f32),
            pltpu.VMEM((dps, ROWS, 2 * LANES), f32),
            pltpu.VMEM((dps, ROWS, 2 * LANES), f32),
            pltpu.VMEM((ROWS, 2 * LANES), f32),
            pltpu.VMEM((dps, seqs, 2 * SUB, LANES), bf16),
            pltpu.VMEM((seqs, SUB, LANES), f32),
            pltpu.VMEM((1, LANES), f32),
            pltpu.VMEM((2 * seqs, SUB, LANES), f32),
            pltpu.VMEM((2 * seqs, 1, LANES), f32),
            pltpu.VMEM((seqs, 2 * SUB, LANES), bf16),
            pltpu.SemaphoreType.DMA((DATA + 1,)),
            pltpu.SemaphoreType.DMA((DATA + pairs,)),
            pltpu.SemaphoreType.DMA((3,)),
            pltpu.SemaphoreType.DMA((9,)),
            pltpu.SemaphoreType.REGULAR,
        ],
        compiler_params=pltpu.CompilerParams(collective_id=0, has_side_effects=True, vmem_limit_bytes=62 << 20),
    )(acts, gate, cot, codes, filter_scales, first, last, forward_table, backward_table, twist)


def finish_kernel(dps, back_ref, grad_ref, rms_ref, cot_ref, filter_scale_ref, input_ref, gate_ref, code_ref, turned, turned_grad):
    step = pl.program_id(0)
    channels = back_ref.shape[0]
    block = channels // dps

    @pl.when(step == 0)
    def _():
        lane = lax.broadcasted_iota(jnp.int32, (1, LANES), 1)
        base = lax.axis_index("dp") * (LANES // dps)

        def decode(i, carry):
            at = pl.ds(i * block, block)
            rms = rms_ref[at]
            tile = back_ref[at].astype(jnp.float32)
            conv = root_of(tile[:, :SUB], 14) * (lane_of(rms, lane, base + CONV_LANE) * (1.0 / TOP14))
            back = root_of(tile[:, SUB:], 8) * (lane_of(rms, lane, base + BACK_LANE) * (1.0 / TOP8_RMS))
            rows = pl.ds(pl.multiple_of(i * block * 2 * SUB, 2 * SUB), block * 2 * SUB)
            turned[rows] = jnp.concatenate([conv, back], axis=1).reshape(block * 2 * SUB, LANES)
            grad = grad_ref[pl.ds(i * (block // 2), block // 2)].astype(jnp.float32).reshape(block, SUB, LANES)
            grad = root_of(grad, 8) * (lane_of(rms, lane, GRAD_LANE) * (1.0 / TOP8_RMS))
            turned_grad[pl.ds(pl.multiple_of(i * block * SUB, SUB), block * SUB)] = grad.reshape(block * SUB, LANES)
            return carry

        lax.fori_loop(0, dps, decode, 0)

    scales = filter_scale_ref[pl.ds(step, 1)]
    for start in range(0, channels, LANES):
        part = slice(start, start + LANES)
        conv = turned[pl.ds(start * 2 * SUB + step, LANES, stride=2 * SUB)].T
        gate_ref[:, part] = (cot_ref[:, part].astype(jnp.float32) * conv).astype(jnp.bfloat16)
        input_ref[:, part] = turned[pl.ds(start * 2 * SUB + SUB + step, LANES, stride=2 * SUB)].T
        grad = turned_grad[pl.ds(start * SUB + step, LANES, stride=SUB)].T
        code_ref[:, part] = grad * scales[:, part]


def finish(dps, back, grad, rms, cot, filter_scales):
    channels = back.shape[0]
    vmem = pl.BlockSpec(memory_space=pltpu.VMEM)
    chunk = pl.BlockSpec((LANES, channels), lambda i: (i, 0))
    return pl.pallas_call(
        functools.partial(finish_kernel, dps),
        grid=(SUB,),
        out_shape=(
            jax.ShapeDtypeStruct(cot.shape, jnp.float32),
            jax.ShapeDtypeStruct(cot.shape, jnp.bfloat16),
            jax.ShapeDtypeStruct(cot.shape, jnp.float32),
        ),
        in_specs=[vmem, vmem, vmem, chunk, vmem],
        out_specs=(chunk,) * 3,
        scratch_shapes=[
            pltpu.VMEM((channels * 2 * SUB, LANES), jnp.float32),
            pltpu.VMEM((channels * SUB, LANES), jnp.float32),
        ],
        compiler_params=pltpu.CompilerParams(vmem_limit_bytes=62 << 20),
    )(back, grad, rms, cot, filter_scales)


def on_device(activations, gate_values, output_grad, filter_codes, filter_scales):
    seqs, dps = lax.axis_size("seq"), lax.axis_size("dp")
    channels = filter_codes.shape[1]
    back, grad, rms = exchange(
        seqs, dps, activations[0], gate_values[0], output_grad[0], filter_codes, filter_scales
    )
    input_grad, gate_grad, code_grad = finish(
        dps, back, grad.reshape(channels // 2, 2 * SUB, LANES), rms.reshape(channels, 1, LANES), output_grad[0], filter_scales
    )
    return (input_grad[None], gate_grad[None], code_grad)


def solution(mesh):
    in_specs = (
        P("dp", "seq", None),
        P("dp", "seq", None),
        P("dp", "seq", None),
        P("seq", None),
        P("seq", None),
    )
    out_specs = (P("dp", "seq", None), P("dp", "seq", None), P("seq", None))
    return jax.shard_map(on_device, mesh=mesh, in_specs=in_specs, out_specs=out_specs, check_vma=False)
```

```python
import functools

import jax
import jax.numpy as jnp
import numpy as np
from jax import lax
from jax.experimental import pallas as pl
from jax.experimental.pallas import tpu as pltpu
from jax.sharding import PartitionSpec as P

LANES = 128
SUB = 8
ROWS = 256
FLOOR = 2.0**-90
TOP8 = 2.0**15
TOP14 = 2.0
TOP8_RMS = 2.0**7.75
RMS_FLOOR = 2.0**-50


def split_np(table):
    high = np.asarray(table, np.float64).astype(jnp.bfloat16)
    low = (np.asarray(table, np.float64) - high.astype(np.float64)).astype(jnp.bfloat16)
    return high, low


def tables():
    whole = 2 * ROWS * LANES
    rows = np.arange(ROWS, dtype=np.float64)
    lanes = np.arange(LANES, dtype=np.float64)
    outer = 2 * np.pi * (rows[:, None] + 0.5) * rows[None, :] / (2 * ROWS)
    first = np.concatenate([np.cos(outer), -np.sin(outer)], axis=0)
    last = np.concatenate([np.cos(outer.T), -np.sin(outer.T)], axis=1) * (2.0 / whole)
    inner = 2 * np.pi * lanes[:, None] * lanes[None, :] / LANES
    cos, sin = np.cos(inner), np.sin(inner)
    forward = np.block([[cos, -sin], [sin, cos]])
    backward = np.block([[cos, sin], [-sin, cos]])
    turn = 2 * np.pi * (rows[:, None] + 0.5) * lanes[None, :] / whole
    twist = np.stack([np.cos(turn), -np.sin(turn)]).astype(np.float32)
    first_hi, first_lo = split_np(first)
    last_hi, last_lo = split_np(last)
    return (
        np.concatenate([first_hi, first_lo], axis=0),
        np.concatenate([last_hi, last_lo], axis=0),
        np.stack(split_np(forward)),
        np.stack(split_np(backward)),
        twist,
    )


def dot(left, right):
    return jnp.dot(left, right, preferred_element_type=jnp.float32)


def halves(value):
    high = value.astype(jnp.bfloat16)
    low = (value - high.astype(jnp.float32)).astype(jnp.bfloat16)
    return high, low


def left_product(table_ref, high, low):
    count = table_ref.shape[0] // 2
    both = dot(table_ref[...], high)
    total = both[:count] + both[count:]
    if low is not None:
        total = total + dot(table_ref[:count], low)
    return total


def right_product(value, table_ref):
    high, low = halves(value)
    return dot(high, table_ref[0]) + dot(low, table_ref[0]) + dot(high, table_ref[1])


def forward(high, low, first_ref, forward_ref, twist_ref):
    section = left_product(first_ref, high, low)
    cos, sin = twist_ref[0], twist_ref[1]
    out = []
    for start in range(0, high.shape[1], LANES):
        real = section[:ROWS, start : start + LANES]
        imag = section[ROWS:, start : start + LANES]
        turned = jnp.concatenate([real * cos - imag * sin, real * sin + imag * cos], axis=1)
        out.append(right_product(turned, forward_ref))
    return out


def inverse(spectra, last_ref, backward_ref, twist_ref):
    cos, sin = twist_ref[0], twist_ref[1]
    sections = []
    for spec in spectra:
        part = right_product(spec, backward_ref)
        real, imag = part[:, :LANES], part[:, LANES:]
        sections.append(jnp.concatenate([real * cos + imag * sin, imag * cos - real * sin], axis=0))
    high, low = halves(jnp.concatenate(sections, axis=1))
    result = left_product(last_ref, high, low)
    return [result[:, i * LANES : (i + 1) * LANES] for i in range(len(spectra))]


def times(left, right):
    lr, li, rr, ri = left[:, :LANES], left[:, LANES:], right[:, :LANES], right[:, LANES:]
    return jnp.concatenate([lr * rr - li * ri, lr * ri + li * rr], axis=1)


def times_conj(left, right):
    lr, li, rr, ri = left[:, :LANES], left[:, LANES:], right[:, :LANES], right[:, LANES:]
    return jnp.concatenate([lr * rr + li * ri, li * rr - lr * ri], axis=1)


def eighth_power(value):
    two = value * value
    four = two * two
    return four * two * value * jnp.abs(value)


def fourteenth_power(value):
    two = value * value
    four = two * two
    return four * four * four * value * jnp.abs(value)


def root_of(code, power):
    size = jnp.exp2(jnp.log2(jnp.abs(code)) * (1.0 / power))
    return jnp.where(code < 0, -size, size)


def root_mean_square(spec):
    whole = 2 * ROWS * LANES
    return jnp.sqrt(jnp.sum(spec * spec, keepdims=True) * (2.0 / whole)) * (1.0 / whole) ** 0.5


def to_peer(source, target, send_sem, recv_sem, seq, dp):
    return pltpu.make_async_remote_copy(
        src_ref=source, dst_ref=target, send_sem=send_sem, recv_sem=recv_sem,
        device_id={"seq": seq, "dp": dp}, device_id_type=pl.DeviceIdType.MESH,
    )


def tell(sem, seq, dp):
    pl.semaphore_signal(sem, inc=1, device_id={"seq": seq, "dp": dp}, device_id_type=pl.DeviceIdType.MESH)


SCALE, TAPS, SCALES, GRAD, RMS, BACK, GRAD_Y, RMS_Y, DATA = range(9)
CONV_LANE, GRAD_LANE, BACK_LANE = 0, 4, 8


AHEAD = 3


def lane_of(rows, lane, wanted):
    return jnp.max(jnp.where(lane == wanted, rows, 0.0), axis=-1, keepdims=True)


def main_kernel(
    seqs, dps, acts_hbm, gate_hbm, cot_hbm, codes_hbm, filter_scale_ref,
    first_hbm, last_hbm, forward_hbm, backward_hbm, twist_hbm,
    back_ref, grad_all_ref, rms_all_ref,
    acts_ref, gate_ref, cot_ref, codes_ref, first_ref, last_ref, forward_ref, backward_ref, twist_ref,
    turned, taps_ref, data_ref, scale_ref,
    got, taps_got, scale_got, scale_row, scales_got, cross_ref, out, grad, rms, held, held_rms,
    grad_code, send_sems, recv_sems, local_sems, load_sems, ready,
):
    seq, dp = lax.axis_index("seq"), lax.axis_index("dp")
    mine = dp * seqs + seq
    pairs = dps // 2
    pair, parity = dp // 2, lax.rem(dp, 2)
    next_seq = lax.rem(seq + 1, seqs)
    lane = lax.broadcasted_iota(jnp.int32, (1, LANES), 1)
    group = LANES // dps
    channels = seqs * dps

    loads = [
        pltpu.make_async_copy(source, target, load_sems.at[i])
        for i, (source, target) in enumerate(
            [(cot_hbm, cot_ref), (gate_hbm, gate_ref), (acts_hbm, acts_ref), (codes_hbm, codes_ref),
             (twist_hbm, twist_ref), (first_hbm, first_ref), (forward_hbm, forward_ref),
             (backward_hbm, backward_ref), (last_hbm, last_ref)]
        )
    ]
    for load in loads:
        load.start()

    def turn():
        for load in loads[:4]:
            load.wait()

        def chunk(i, top):
            at = pl.ds(pl.multiple_of(i * LANES, LANES), LANES)
            acts = acts_ref[at].astype(jnp.float32)
            grads = cot_ref[at].astype(jnp.float32) * gate_ref[at].astype(jnp.float32)
            taps = codes_ref[at].astype(jnp.float32) * filter_scale_ref[pl.ds(i, 1)]
            for start in range(0, channels, LANES):
                part = slice(start, start + LANES)
                turned[pl.ds(start * 2 * SUB + i, LANES, stride=2 * SUB)] = acts[:, part].T
                turned[pl.ds(start * 2 * SUB + SUB + i, LANES, stride=2 * SUB)] = grads[:, part].T
                taps_ref[pl.ds(start * SUB + i, LANES, stride=SUB)] = taps[:, part].T
            return jnp.maximum(top, jnp.max(jnp.abs(grads), axis=0, keepdims=True))

        top = lax.fori_loop(0, SUB, chunk, jnp.zeros((1, channels), jnp.float32))
        top = jnp.maximum(jnp.max(top, keepdims=True), FLOOR)
        scale_ref[...] = jnp.broadcast_to(top * (1.0 / TOP8), (1, LANES))
        factor = (TOP8 / top).reshape(1, 1, 1)

        def code(i, carry):
            tile = turned[pl.ds(pl.multiple_of(i * seqs * 2 * SUB, 2 * SUB), seqs * 2 * SUB)]
            tile = tile.reshape(seqs, 2 * SUB, LANES)
            coded = jnp.concatenate([tile[:, :SUB], eighth_power(tile[:, SUB:] * factor)], axis=1)
            data_ref[pl.ds(i * seqs, seqs)] = coded.astype(jnp.bfloat16)
            return carry

        lax.fori_loop(0, dps, code, 0)

    def copy_to(source, target, kind, seq_to, dp_to, recv_kind=None):
        return to_peer(
            source, target, send_sems.at[kind], recv_sems.at[kind if recv_kind is None else recv_kind], seq_to, dp_to
        )

    def of(ref, count, kind, recv_kind=None):
        part = ref.at[pl.ds(0, count)]
        return copy_to(part, part, kind, next_seq, dp, recv_kind)

    def taps_of(seq_to):
        return taps_ref.at[pl.ds(pl.multiple_of((dp * seqs + seq_to) * SUB, SUB), SUB)]

    barrier = pltpu.get_barrier_semaphore()

    def tell_pair(offset, carry):
        tell(barrier, lax.rem(seq + offset // 2, seqs), pair * 2 + lax.rem(parity + offset, 2))
        return carry

    def tell_others(sem):
        def body(offset, carry):
            tell(sem, seq, lax.rem(pair + offset, pairs) * 2 + parity)
            return carry

        return body

    lax.fori_loop(1, pairs, tell_others(barrier), 0)
    lax.fori_loop(1, 2 * seqs, tell_pair, 0)
    turn()
    pl.semaphore_wait(barrier, 2 * seqs + pairs - 2)
    lax.fori_loop(1, pairs, tell_others(ready), 0)

    def send_scale(offset, carry):
        copy_to(scale_ref, scale_got.at[dp], SCALE, seq, lax.rem(dp + offset, dps)).start()
        return carry

    def send_taps(offset, carry):
        peer = lax.rem(seq + offset, seqs)
        copy_to(taps_of(peer), taps_got.at[seq], TAPS, peer, dp).start()
        return carry

    lax.fori_loop(1, seqs, send_taps, 0)

    def send_pair(step, source_of, target, kind, recv_kind):
        peer_pair = lax.rem(pair + step, pairs)

        def send(offset, carry):
            peer_seq = lax.rem(seq + offset // 2, seqs)
            peer_dp = peer_pair * 2 + lax.rem(parity + offset, 2)
            copy_to(source_of(peer_seq, peer_dp), target.at[mine], kind, peer_seq, peer_dp, recv_kind).start()
            return carry

        lax.fori_loop(jnp.where(lax.rem(step, pairs) == 0, 1, 0), 2 * seqs, send, 0)

    def send_data(step):
        send_pair(step, lambda s, d: data_ref.at[d * seqs + s], got, DATA + step, DATA + pair)

    def sent_data(step, count):
        of(got, count, DATA + step, DATA + step).wait_send()

    send_data(0)
    pl.semaphore_wait(ready, pairs - 1)
    lax.fori_loop(1, dps, send_scale, 0)
    lax.fori_loop(1, AHEAD, lambda step, carry: (send_data(step), carry)[1], 0)
    own = pltpu.make_async_copy(data_ref.at[mine], got.at[mine], local_sems.at[0])
    own.start()
    own_taps = pltpu.make_async_copy(taps_of(seq), taps_got.at[seq], local_sems.at[1])
    own_taps.start()

    of(scale_got, dps - 1, SCALE).wait()
    scale_got[dp] = scale_ref[...]
    row = jnp.zeros((1, LANES), jnp.float32)
    for other in range(dps):
        row = jnp.where(lane // group == other, scale_got[other], row)
    scale_row[...] = row

    def send_row(offset, carry):
        copy_to(scale_row, scales_got.at[seq], SCALES, lax.rem(seq + offset, seqs), dp).start()
        return carry

    lax.fori_loop(1, seqs, send_row, 0)

    for load in loads[4:]:
        load.wait()
    own_taps.wait()
    of(taps_got, seqs - 1, TAPS).wait()
    taps_high, taps_low = halves(taps_got[...].reshape(ROWS, LANES))
    (taps_spec,) = forward(taps_high, taps_low, first_ref, forward_ref, twist_ref)
    cross_ref[...] = jnp.zeros_like(cross_ref)
    own.wait()
    of(scales_got, seqs - 1, SCALES).wait()
    scales_got[seq] = scale_row[...]
    of(got, 2 * seqs - 1, DATA, DATA + pair).wait_recv()
    rms[...] = jnp.zeros_like(rms)

    def send_back(step):
        send_pair(pairs - step, lambda s, d: out.at[d, s], back_ref, BACK, BACK)

    def send_grads():
        cross = cross_ref[...]
        grad_rms = jnp.maximum(root_mean_square(cross), RMS_FLOOR)
        in_group = lane % group
        rms[...] = jnp.where((in_group >= GRAD_LANE) & (in_group < BACK_LANE), grad_rms, rms[...])
        (grad_value,) = inverse([cross], last_ref, backward_ref, twist_ref)
        grad[...] = grad_value.reshape(seqs, SUB, LANES)

        def send_grad(offset, carry):
            peer_seq = lax.rem(seq + offset // 2, seqs)
            peer_dp = pair * 2 + lax.rem(parity + offset, 2)
            copy_to(grad.at[peer_seq], held.at[parity * seqs + seq], GRAD, peer_seq, peer_dp).start()
            copy_to(rms, held_rms.at[parity * seqs + seq], RMS, peer_seq, peer_dp).start()
            return carry

        lax.fori_loop(1, 2 * seqs, send_grad, 0)

    def transform_pair(step, carry):
        source = lax.rem(pair + pairs - step, pairs)

        @pl.when(step > 0)
        def _():
            of(got, 2 * seqs, DATA, DATA + source).wait_recv()

        @pl.when(step == 0)
        def _():
            sent_data(step, 2 * seqs - 1)

        @pl.when(step < pairs - AHEAD)
        def _():
            send_data(step + AHEAD)

        signals, acts = [], []
        for half in range(2):
            index = source * 2 + half
            tile = got[pl.ds(index * seqs, seqs)].astype(jnp.float32)
            signals.append(tile[:, :SUB].reshape(ROWS, LANES).astype(jnp.bfloat16))
            scale = lane_of(scales_got[...], lane, index * group)
            acts.append((root_of(tile[:, SUB:], 8) * scale).reshape(ROWS, LANES))
        act_high, act_low = halves(jnp.concatenate(acts, axis=1))
        signal_specs = forward(jnp.concatenate(signals, axis=1), None, first_ref, forward_ref, twist_ref)
        act_specs = forward(act_high, act_low, first_ref, forward_ref, twist_ref)
        conv_specs, back_specs, factors = [], [], []
        for half, (signal_spec, act_spec) in enumerate(zip(signal_specs, act_specs)):
            index = source * 2 + half
            cross_ref[...] += times_conj(act_spec, signal_spec)
            conv_spec, back_spec = times(signal_spec, carry), times_conj(act_spec, carry)
            conv_specs.append(conv_spec)
            back_specs.append(back_spec)
            conv_rms = jnp.maximum(root_mean_square(conv_spec), RMS_FLOOR)
            back_rms = jnp.maximum(root_mean_square(back_spec), RMS_FLOOR)
            factors.append((TOP14 / conv_rms, TOP8_RMS / back_rms))
            both = jnp.where(lane % group < BACK_LANE, conv_rms, back_rms)
            rms[...] = jnp.where(lane // group == index, both, rms[...])

        @pl.when(step == pairs - 1)
        def _():
            send_grads()
            send_back(1)
            send_back(2)

        convs = inverse(conv_specs, last_ref, backward_ref, twist_ref)
        backs = inverse(back_specs, last_ref, backward_ref, twist_ref)
        for half in range(2):
            conv_code = fourteenth_power(convs[half] * factors[half][0]).reshape(seqs, SUB, LANES)
            back_code = eighth_power(backs[half] * factors[half][1]).reshape(seqs, SUB, LANES)
            out[source * 2 + half] = jnp.concatenate([conv_code, back_code], axis=1).astype(jnp.bfloat16)

        @pl.when(step == 0)
        def _():
            send_back(step)

        return carry

    lax.fori_loop(0, pairs, transform_pair, taps_spec)
    own_back = pltpu.make_async_copy(out.at[dp, seq], back_ref.at[mine], local_sems.at[0])
    own_back.start()

    of(held, 2 * seqs - 1, GRAD).wait()
    of(held_rms, 2 * seqs - 1, RMS).wait()
    held[parity * seqs + seq] = grad[seq]
    held_rms[parity * seqs + seq] = rms[...]
    code = eighth_power(held[...] * (TOP8_RMS / lane_of(held_rms[...], lane, GRAD_LANE)))
    grad_code[...] = code.reshape(seqs, 2 * SUB, LANES).astype(jnp.bfloat16)

    def send_along(offset, carry):
        peer_dp = lax.rem(pair + offset, pairs) * 2 + parity
        copy_to(grad_code, grad_all_ref.at[pair], GRAD_Y, seq, peer_dp).start()
        copy_to(held_rms, rms_all_ref.at[pair], RMS_Y, seq, peer_dp).start()
        return carry

    lax.fori_loop(1, pairs, send_along, 0)
    lax.fori_loop(3, pairs, lambda step, carry: (send_back(step), carry)[1], 0)
    own_grad = pltpu.make_async_copy(grad_code, grad_all_ref.at[pair], local_sems.at[1])
    own_grad.start()
    own_rms = pltpu.make_async_copy(held_rms, rms_all_ref.at[pair], local_sems.at[2])
    own_rms.start()
    own_back.wait()
    own_grad.wait()
    own_rms.wait()
    lax.fori_loop(pairs - AHEAD, pairs, lambda step, carry: (sent_data(step, 2 * seqs), carry)[1], 0)
    of(grad_all_ref, pairs - 1, GRAD_Y).wait()
    of(rms_all_ref, pairs - 1, RMS_Y).wait()
    of(back_ref, channels - 1, BACK).wait()


def exchange(seqs, dps, acts, gate, cot, codes, filter_scales):
    pairs, channels = dps // 2, seqs * dps
    vmem, hbm = pl.BlockSpec(memory_space=pltpu.VMEM), pl.BlockSpec(memory_space=pl.ANY)
    f32, bf16 = jnp.float32, jnp.bfloat16
    constants = [jnp.asarray(t) for t in tables()]
    first, last, forward_table, backward_table, twist = constants
    return pl.pallas_call(
        functools.partial(main_kernel, seqs, dps),
        out_shape=(
            jax.ShapeDtypeStruct((channels, 2 * SUB, LANES), bf16),
            jax.ShapeDtypeStruct((pairs, seqs, 2 * SUB, LANES), bf16),
            jax.ShapeDtypeStruct((pairs, 2 * seqs, 1, LANES), f32),
        ),
        in_specs=[hbm] * 4 + [vmem] + [hbm] * 5,
        out_specs=(vmem,) * 3,
        scratch_shapes=[pltpu.VMEM(value.shape, bf16) for value in (acts, gate, cot, codes)]
        + [pltpu.VMEM(value.shape, value.dtype) for value in constants]
        + [
            pltpu.VMEM((channels * 2 * SUB, LANES), f32),
            pltpu.VMEM((channels * SUB, LANES), f32),
            pltpu.VMEM((channels, 2 * SUB, LANES), bf16),
            pltpu.VMEM((1, LANES), f32),
            pltpu.VMEM((channels, 2 * SUB, LANES), bf16),
            pltpu.VMEM((seqs, SUB, LANES), f32),
            pltpu.VMEM((dps, 1, LANES), f32),
            pltpu.VMEM((1, LANES), f32),
            pltpu.VMEM((seqs, 1, LANES), f32),
            pltpu.VMEM((ROWS, 2 * LANES), f32),
            pltpu.VMEM((dps, seqs, 2 * SUB, LANES), bf16),
            pltpu.VMEM((seqs, SUB, LANES), f32),
            pltpu.VMEM((1, LANES), f32),
            pltpu.VMEM((2 * seqs, SUB, LANES), f32),
            pltpu.VMEM((2 * seqs, 1, LANES), f32),
            pltpu.VMEM((seqs, 2 * SUB, LANES), bf16),
            pltpu.SemaphoreType.DMA((DATA + pairs,)),
            pltpu.SemaphoreType.DMA((DATA + pairs,)),
            pltpu.SemaphoreType.DMA((3,)),
            pltpu.SemaphoreType.DMA((9,)),
            pltpu.SemaphoreType.REGULAR,
        ],
        compiler_params=pltpu.CompilerParams(collective_id=0, has_side_effects=True, vmem_limit_bytes=62 << 20),
    )(acts, gate, cot, codes, filter_scales, first, last, forward_table, backward_table, twist)


def finish_kernel(dps, back_ref, grad_ref, rms_ref, cot_ref, filter_scale_ref, input_ref, gate_ref, code_ref, turned, turned_grad):
    step = pl.program_id(0)
    channels = back_ref.shape[0]
    block = channels // dps

    @pl.when(step == 0)
    def _():
        lane = lax.broadcasted_iota(jnp.int32, (1, LANES), 1)
        base = lax.axis_index("dp") * (LANES // dps)

        def decode(i, carry):
            at = pl.ds(i * block, block)
            rms = rms_ref[at]
            tile = back_ref[at].astype(jnp.float32)
            conv = root_of(tile[:, :SUB], 14) * (lane_of(rms, lane, base + CONV_LANE) * (1.0 / TOP14))
            back = root_of(tile[:, SUB:], 8) * (lane_of(rms, lane, base + BACK_LANE) * (1.0 / TOP8_RMS))
            rows = pl.ds(pl.multiple_of(i * block * 2 * SUB, 2 * SUB), block * 2 * SUB)
            turned[rows] = jnp.concatenate([conv, back], axis=1).reshape(block * 2 * SUB, LANES)
            grad = grad_ref[pl.ds(i * (block // 2), block // 2)].astype(jnp.float32).reshape(block, SUB, LANES)
            grad = root_of(grad, 8) * (lane_of(rms, lane, GRAD_LANE) * (1.0 / TOP8_RMS))
            turned_grad[pl.ds(pl.multiple_of(i * block * SUB, SUB), block * SUB)] = grad.reshape(block * SUB, LANES)
            return carry

        lax.fori_loop(0, dps, decode, 0)

    scales = filter_scale_ref[pl.ds(step, 1)]
    for start in range(0, channels, LANES):
        part = slice(start, start + LANES)
        conv = turned[pl.ds(start * 2 * SUB + step, LANES, stride=2 * SUB)].T
        gate_ref[:, part] = (cot_ref[:, part].astype(jnp.float32) * conv).astype(jnp.bfloat16)
        input_ref[:, part] = turned[pl.ds(start * 2 * SUB + SUB + step, LANES, stride=2 * SUB)].T
        grad = turned_grad[pl.ds(start * SUB + step, LANES, stride=SUB)].T
        code_ref[:, part] = grad * scales[:, part]


def finish(dps, back, grad, rms, cot, filter_scales):
    channels = back.shape[0]
    vmem = pl.BlockSpec(memory_space=pltpu.VMEM)
    chunk = pl.BlockSpec((LANES, channels), lambda i: (i, 0))
    return pl.pallas_call(
        functools.partial(finish_kernel, dps),
        grid=(SUB,),
        out_shape=(
            jax.ShapeDtypeStruct(cot.shape, jnp.float32),
            jax.ShapeDtypeStruct(cot.shape, jnp.bfloat16),
            jax.ShapeDtypeStruct(cot.shape, jnp.float32),
        ),
        in_specs=[vmem, vmem, vmem, chunk, vmem],
        out_specs=(chunk,) * 3,
        scratch_shapes=[
            pltpu.VMEM((channels * 2 * SUB, LANES), jnp.float32),
            pltpu.VMEM((channels * SUB, LANES), jnp.float32),
        ],
        compiler_params=pltpu.CompilerParams(vmem_limit_bytes=62 << 20),
    )(back, grad, rms, cot, filter_scales)


def on_device(activations, gate_values, output_grad, filter_codes, filter_scales):
    seqs, dps = lax.axis_size("seq"), lax.axis_size("dp")
    channels = filter_codes.shape[1]
    back, grad, rms = exchange(
        seqs, dps, activations[0], gate_values[0], output_grad[0], filter_codes, filter_scales
    )
    input_grad, gate_grad, code_grad = finish(
        dps, back, grad.reshape(channels // 2, 2 * SUB, LANES), rms.reshape(channels, 1, LANES), output_grad[0], filter_scales
    )
    return (input_grad[None], gate_grad[None], code_grad)


def solution(mesh):
    in_specs = (
        P("dp", "seq", None),
        P("dp", "seq", None),
        P("dp", "seq", None),
        P("seq", None),
        P("seq", None),
    )
    out_specs = (P("dp", "seq", None), P("dp", "seq", None), P("seq", None))
    return jax.shard_map(on_device, mesh=mesh, in_specs=in_specs, out_specs=out_specs, check_vma=False)
```

```python
import functools

import jax
import jax.numpy as jnp
import numpy as np
from jax import lax
from jax.experimental import pallas as pl
from jax.experimental.pallas import tpu as pltpu
from jax.sharding import PartitionSpec as P

LANES = 128
SUB = 8
ROWS = 256
FLOOR = 2.0**-90
TOP8 = 2.0**15
TOP14 = 2.0
TOP8_RMS = 2.0**7.75
RMS_FLOOR = 2.0**-50


def split_np(table):
    high = np.asarray(table, np.float64).astype(jnp.bfloat16)
    low = (np.asarray(table, np.float64) - high.astype(np.float64)).astype(jnp.bfloat16)
    return high, low


def tables():
    whole = 2 * ROWS * LANES
    rows = np.arange(ROWS, dtype=np.float64)
    lanes = np.arange(LANES, dtype=np.float64)
    outer = 2 * np.pi * (rows[:, None] + 0.5) * rows[None, :] / (2 * ROWS)
    first = np.concatenate([np.cos(outer), -np.sin(outer)], axis=0)
    last = np.concatenate([np.cos(outer.T), -np.sin(outer.T)], axis=1) * (2.0 / whole)
    inner = 2 * np.pi * lanes[:, None] * lanes[None, :] / LANES
    cos, sin = np.cos(inner), np.sin(inner)
    forward = np.block([[cos, -sin], [sin, cos]])
    backward = np.block([[cos, sin], [-sin, cos]])
    turn = 2 * np.pi * (rows[:, None] + 0.5) * lanes[None, :] / whole
    twist = np.stack([np.cos(turn), -np.sin(turn)]).astype(np.float32)
    first_hi, first_lo = split_np(first)
    last_hi, last_lo = split_np(last)
    return (
        np.concatenate([first_hi, first_lo], axis=0),
        np.concatenate([last_hi, last_lo], axis=0),
        np.stack(split_np(forward)),
        np.stack(split_np(backward)),
        twist,
    )


def dot(left, right):
    return jnp.dot(left, right, preferred_element_type=jnp.float32)


def halves(value):
    high = value.astype(jnp.bfloat16)
    low = (value - high.astype(jnp.float32)).astype(jnp.bfloat16)
    return high, low


def left_product(table_ref, high, low):
    count = table_ref.shape[0] // 2
    both = dot(table_ref[...], high)
    total = both[:count] + both[count:]
    if low is not None:
        total = total + dot(table_ref[:count], low)
    return total


def right_product(value, table_ref):
    high, low = halves(value)
    return dot(high, table_ref[0]) + dot(low, table_ref[0]) + dot(high, table_ref[1])


def forward(high, low, first_ref, forward_ref, twist_ref):
    section = left_product(first_ref, high, low)
    cos, sin = twist_ref[0], twist_ref[1]
    out = []
    for start in range(0, high.shape[1], LANES):
        real = section[:ROWS, start : start + LANES]
        imag = section[ROWS:, start : start + LANES]
        turned = jnp.concatenate([real * cos - imag * sin, real * sin + imag * cos], axis=1)
        out.append(right_product(turned, forward_ref))
    return out


def inverse(spectra, last_ref, backward_ref, twist_ref):
    cos, sin = twist_ref[0], twist_ref[1]
    sections = []
    for spec in spectra:
        part = right_product(spec, backward_ref)
        real, imag = part[:, :LANES], part[:, LANES:]
        sections.append(jnp.concatenate([real * cos + imag * sin, imag * cos - real * sin], axis=0))
    high, low = halves(jnp.concatenate(sections, axis=1))
    result = left_product(last_ref, high, low)
    return [result[:, i * LANES : (i + 1) * LANES] for i in range(len(spectra))]


def times(left, right):
    lr, li, rr, ri = left[:, :LANES], left[:, LANES:], right[:, :LANES], right[:, LANES:]
    return jnp.concatenate([lr * rr - li * ri, lr * ri + li * rr], axis=1)


def times_conj(left, right):
    lr, li, rr, ri = left[:, :LANES], left[:, LANES:], right[:, :LANES], right[:, LANES:]
    return jnp.concatenate([lr * rr + li * ri, li * rr - lr * ri], axis=1)


def eighth_power(value):
    two = value * value
    four = two * two
    return four * two * value * jnp.abs(value)


def fourteenth_power(value):
    two = value * value
    four = two * two
    return four * four * four * value * jnp.abs(value)


def root_of(code, power):
    size = jnp.exp2(jnp.log2(jnp.abs(code)) * (1.0 / power))
    return jnp.where(code < 0, -size, size)


def root_mean_square(spec):
    whole = 2 * ROWS * LANES
    return jnp.sqrt(jnp.sum(spec * spec, keepdims=True) * (2.0 / whole)) * (1.0 / whole) ** 0.5


def to_peer(source, target, send_sem, recv_sem, seq, dp):
    return pltpu.make_async_remote_copy(
        src_ref=source, dst_ref=target, send_sem=send_sem, recv_sem=recv_sem,
        device_id={"seq": seq, "dp": dp}, device_id_type=pl.DeviceIdType.MESH,
    )


def tell(sem, seq, dp):
    pl.semaphore_signal(sem, inc=1, device_id={"seq": seq, "dp": dp}, device_id_type=pl.DeviceIdType.MESH)


SCALE, TAPS, SCALES, GRAD, RMS, BACK, GRAD_Y, RMS_Y, DATA = range(9)
CONV_LANE, GRAD_LANE, BACK_LANE = 0, 4, 8


AHEAD = 3


BLOCK = 32


def lane_of(rows, lane, wanted):
    return jnp.max(jnp.where(lane == wanted, rows, 0.0), axis=-1, keepdims=True)


def main_kernel(
    seqs, dps, acts_hbm, gate_hbm, cot_hbm, codes_hbm, filter_scale_ref,
    first_hbm, last_hbm, forward_hbm, backward_hbm, twist_hbm,
    back_ref, grad_all_ref, rms_all_ref,
    acts_ref, gate_ref, cot_ref, codes_ref, first_ref, last_ref, forward_ref, backward_ref, twist_ref,
    turned, taps_ref, data_ref, scale_ref,
    got, taps_got, scale_got, scale_row, scales_got, cross_ref, out, grad, rms, held, held_rms,
    grad_code, send_sems, recv_sems, local_sems, load_sems, ready,
):
    seq, dp = lax.axis_index("seq"), lax.axis_index("dp")
    mine = dp * seqs + seq
    pairs = dps // 2
    pair, parity = dp // 2, lax.rem(dp, 2)
    next_seq = lax.rem(seq + 1, seqs)
    lane = lax.broadcasted_iota(jnp.int32, (1, LANES), 1)
    group = LANES // dps
    channels = seqs * dps

    loads = [
        pltpu.make_async_copy(source, target, load_sems.at[i])
        for i, (source, target) in enumerate(
            [(cot_hbm, cot_ref), (gate_hbm, gate_ref), (acts_hbm, acts_ref), (codes_hbm, codes_ref),
             (twist_hbm, twist_ref), (first_hbm, first_ref), (forward_hbm, forward_ref),
             (backward_hbm, backward_ref), (last_hbm, last_ref)]
        )
    ]
    for load in loads:
        load.start()

    def turn():
        for load in loads[:4]:
            load.wait()

        def chunk(i, top):
            at = pl.ds(pl.multiple_of(i * LANES, LANES), LANES)
            acts = acts_ref[at].astype(jnp.float32)
            grads = cot_ref[at].astype(jnp.float32) * gate_ref[at].astype(jnp.float32)
            taps = codes_ref[at].astype(jnp.float32) * filter_scale_ref[pl.ds(i, 1)]
            for start in range(0, channels, LANES):
                part = slice(start, start + LANES)
                turned[pl.ds(start * 2 * SUB + i, LANES, stride=2 * SUB)] = acts[:, part].T
                turned[pl.ds(start * 2 * SUB + SUB + i, LANES, stride=2 * SUB)] = grads[:, part].T
                taps_ref[pl.ds(start * SUB + i, LANES, stride=SUB)] = taps[:, part].T
            return jnp.maximum(top, jnp.max(jnp.abs(grads), axis=0, keepdims=True))

        top = lax.fori_loop(0, SUB, chunk, jnp.zeros((1, channels), jnp.float32))
        top = jnp.maximum(jnp.max(top, keepdims=True), FLOOR)
        scale_ref[...] = jnp.broadcast_to(top * (1.0 / TOP8), (1, LANES))
        factor = (TOP8 / top).reshape(1, 1, 1)

        def code(i, carry):
            tile = turned[pl.ds(pl.multiple_of(i * seqs * 2 * SUB, 2 * SUB), seqs * 2 * SUB)]
            tile = tile.reshape(seqs, 2 * SUB, LANES)
            coded = jnp.concatenate([tile[:, :SUB], eighth_power(tile[:, SUB:] * factor)], axis=1)
            data_ref[pl.ds(i * seqs, seqs)] = coded.astype(jnp.bfloat16)
            return carry

        lax.fori_loop(0, dps, code, 0)

    def copy_to(source, target, kind, seq_to, dp_to, recv_kind=None):
        return to_peer(
            source, target, send_sems.at[kind], recv_sems.at[kind if recv_kind is None else recv_kind], seq_to, dp_to
        )

    def of(ref, count, kind, recv_kind=None):
        part = ref.at[pl.ds(0, count)]
        return copy_to(part, part, kind, next_seq, dp, recv_kind)

    def taps_of(seq_to):
        return taps_ref.at[pl.ds(pl.multiple_of((dp * seqs + seq_to) * SUB, SUB), SUB)]

    barrier = pltpu.get_barrier_semaphore()

    def tell_pair(offset, carry):
        tell(barrier, lax.rem(seq + offset // 2, seqs), pair * 2 + lax.rem(parity + offset, 2))
        return carry

    def tell_others(sem):
        def body(offset, carry):
            tell(sem, seq, lax.rem(pair + offset, pairs) * 2 + parity)
            return carry

        return body

    lax.fori_loop(1, pairs, tell_others(barrier), 0)
    lax.fori_loop(1, 2 * seqs, tell_pair, 0)
    turn()
    pl.semaphore_wait(barrier, 2 * seqs + pairs - 2)
    lax.fori_loop(1, pairs, tell_others(ready), 0)

    def send_scale(offset, carry):
        copy_to(scale_ref, scale_got.at[dp], SCALE, seq, lax.rem(dp + offset, dps)).start()
        return carry

    def send_taps(offset, carry):
        peer = lax.rem(seq + offset, seqs)
        copy_to(taps_of(peer), taps_got.at[seq], TAPS, peer, dp).start()
        return carry

    lax.fori_loop(1, seqs, send_taps, 0)

    def send_pair(step, source_of, target, kind, recv_kind):
        peer_pair = lax.rem(pair + step, pairs)

        def send(offset, carry):
            peer_seq = lax.rem(seq + offset // 2, seqs)
            peer_dp = peer_pair * 2 + lax.rem(parity + offset, 2)
            copy_to(source_of(peer_seq, peer_dp), target.at[mine], kind, peer_seq, peer_dp, recv_kind).start()
            return carry

        lax.fori_loop(jnp.where(lax.rem(step, pairs) == 0, 1, 0), 2 * seqs, send, 0)

    def send_data(step):
        send_pair(step, lambda s, d: data_ref.at[d * seqs + s], got, DATA + step, DATA + pair)

    def sent_data(step, count):
        of(got, count, DATA + step, DATA + step).wait_send()

    send_data(0)
    pl.semaphore_wait(ready, pairs - 1)
    lax.fori_loop(1, dps, send_scale, 0)
    lax.fori_loop(1, AHEAD, lambda step, carry: (send_data(step), carry)[1], 0)
    own = pltpu.make_async_copy(data_ref.at[mine], got.at[mine], local_sems.at[0])
    own.start()
    own_taps = pltpu.make_async_copy(taps_of(seq), taps_got.at[seq], local_sems.at[1])
    own_taps.start()

    of(scale_got, dps - 1, SCALE).wait()
    scale_got[dp] = scale_ref[...]
    row = jnp.zeros((1, LANES), jnp.float32)
    for other in range(dps):
        row = jnp.where(lane // group == other, scale_got[other], row)
    scale_row[...] = row

    def send_row(offset, carry):
        copy_to(scale_row, scales_got.at[seq], SCALES, lax.rem(seq + offset, seqs), dp).start()
        return carry

    lax.fori_loop(1, seqs, send_row, 0)

    for load in loads[4:]:
        load.wait()
    own_taps.wait()
    of(taps_got, seqs - 1, TAPS).wait()
    taps_high, taps_low = halves(taps_got[...].reshape(ROWS, LANES))
    (taps_spec,) = forward(taps_high, taps_low, first_ref, forward_ref, twist_ref)
    cross_ref[...] = jnp.zeros_like(cross_ref)
    own.wait()
    of(scales_got, seqs - 1, SCALES).wait()
    scales_got[seq] = scale_row[...]
    of(got, 2 * seqs - 1, DATA, DATA + pair).wait_recv()
    rms[...] = jnp.zeros_like(rms)

    def send_back(step):
        send_pair(pairs - step, lambda s, d: out.at[d, s], back_ref, BACK, BACK)

    def send_grads():
        cross = cross_ref[...]
        grad_rms = jnp.maximum(root_mean_square(cross), RMS_FLOOR)
        in_group = lane % group
        rms[...] = jnp.where((in_group >= GRAD_LANE) & (in_group < BACK_LANE), grad_rms, rms[...])
        (grad_value,) = inverse([cross], last_ref, backward_ref, twist_ref)
        grad[...] = grad_value.reshape(seqs, SUB, LANES)

        def send_grad(offset, carry):
            peer_seq = lax.rem(seq + offset // 2, seqs)
            peer_dp = pair * 2 + lax.rem(parity + offset, 2)
            copy_to(grad.at[peer_seq], held.at[parity * seqs + seq], GRAD, peer_seq, peer_dp).start()
            copy_to(rms, held_rms.at[parity * seqs + seq], RMS, peer_seq, peer_dp).start()
            return carry

        lax.fori_loop(1, 2 * seqs, send_grad, 0)

    def transform_pair(step, carry):
        source = lax.rem(pair + pairs - step, pairs)

        @pl.when(step > 0)
        def _():
            of(got, 2 * seqs, DATA, DATA + source).wait_recv()

        @pl.when(step == 0)
        def _():
            sent_data(step, 2 * seqs - 1)

        @pl.when(step < pairs - AHEAD)
        def _():
            send_data(step + AHEAD)

        signals, acts = [], []
        for half in range(2):
            index = source * 2 + half
            tile = got[pl.ds(index * seqs, seqs)].astype(jnp.float32)
            signals.append(tile[:, :SUB].reshape(ROWS, LANES).astype(jnp.bfloat16))
            scale = lane_of(scales_got[...], lane, index * group)
            acts.append((root_of(tile[:, SUB:], 8) * scale).reshape(ROWS, LANES))
        act_high, act_low = halves(jnp.concatenate(acts, axis=1))
        signal_specs = forward(jnp.concatenate(signals, axis=1), None, first_ref, forward_ref, twist_ref)
        act_specs = forward(act_high, act_low, first_ref, forward_ref, twist_ref)
        conv_specs, back_specs, factors = [], [], []
        for half, (signal_spec, act_spec) in enumerate(zip(signal_specs, act_specs)):
            index = source * 2 + half
            cross_ref[...] += times_conj(act_spec, signal_spec)
            conv_spec, back_spec = times(signal_spec, carry), times_conj(act_spec, carry)
            conv_specs.append(conv_spec)
            back_specs.append(back_spec)
            conv_rms = jnp.maximum(root_mean_square(conv_spec), RMS_FLOOR)
            back_rms = jnp.maximum(root_mean_square(back_spec), RMS_FLOOR)
            factors.append((TOP14 / conv_rms, TOP8_RMS / back_rms))
            both = jnp.where(lane % group < BACK_LANE, conv_rms, back_rms)
            rms[...] = jnp.where(lane // group == index, both, rms[...])

        @pl.when(step == pairs - 1)
        def _():
            send_grads()
            send_back(1)
            send_back(2)

        convs = inverse(conv_specs, last_ref, backward_ref, twist_ref)
        backs = inverse(back_specs, last_ref, backward_ref, twist_ref)
        for half in range(2):
            conv_code = fourteenth_power(convs[half] * factors[half][0]).reshape(seqs, SUB, LANES)
            back_code = eighth_power(backs[half] * factors[half][1]).reshape(seqs, SUB, LANES)
            out[source * 2 + half] = jnp.concatenate([conv_code, back_code], axis=1).astype(jnp.bfloat16)

        @pl.when(step == 0)
        def _():
            send_back(step)

        return carry

    lax.fori_loop(0, pairs, transform_pair, taps_spec)
    own_back = pltpu.make_async_copy(out.at[dp, seq], back_ref.at[mine], local_sems.at[0])
    own_back.start()

    of(held, 2 * seqs - 1, GRAD).wait()
    of(held_rms, 2 * seqs - 1, RMS).wait()
    held[parity * seqs + seq] = grad[seq]
    held_rms[parity * seqs + seq] = rms[...]
    code = eighth_power(held[...] * (TOP8_RMS / lane_of(held_rms[...], lane, GRAD_LANE)))
    grad_code[...] = code.reshape(seqs, 2 * SUB, LANES).astype(jnp.bfloat16)

    def send_along(offset, carry):
        peer_dp = lax.rem(pair + offset, pairs) * 2 + parity
        copy_to(grad_code, grad_all_ref.at[pair], GRAD_Y, seq, peer_dp).start()
        copy_to(held_rms, rms_all_ref.at[pair], RMS_Y, seq, peer_dp).start()
        return carry

    lax.fori_loop(1, pairs, send_along, 0)
    lax.fori_loop(3, pairs, lambda step, carry: (send_back(step), carry)[1], 0)
    own_grad = pltpu.make_async_copy(grad_code, grad_all_ref.at[pair], local_sems.at[1])
    own_grad.start()
    own_rms = pltpu.make_async_copy(held_rms, rms_all_ref.at[pair], local_sems.at[2])
    own_rms.start()
    own_back.wait()
    own_grad.wait()
    own_rms.wait()
    lax.fori_loop(pairs - AHEAD, pairs, lambda step, carry: (sent_data(step, 2 * seqs), carry)[1], 0)
    of(grad_all_ref, pairs - 1, GRAD_Y).wait()
    of(rms_all_ref, pairs - 1, RMS_Y).wait()
    of(back_ref, channels - 1, BACK).wait()


def exchange(seqs, dps, acts, gate, cot, codes, filter_scales):
    pairs, channels = dps // 2, seqs * dps
    vmem, hbm = pl.BlockSpec(memory_space=pltpu.VMEM), pl.BlockSpec(memory_space=pl.ANY)
    f32, bf16 = jnp.float32, jnp.bfloat16
    constants = [jnp.asarray(t) for t in tables()]
    first, last, forward_table, backward_table, twist = constants
    return pl.pallas_call(
        functools.partial(main_kernel, seqs, dps),
        out_shape=(
            jax.ShapeDtypeStruct((channels, 2 * SUB, LANES), bf16),
            jax.ShapeDtypeStruct((pairs, seqs, 2 * SUB, LANES), bf16),
            jax.ShapeDtypeStruct((pairs, 2 * seqs, 1, LANES), f32),
        ),
        in_specs=[hbm] * 4 + [vmem] + [hbm] * 5,
        out_specs=(vmem,) * 3,
        scratch_shapes=[pltpu.VMEM(value.shape, bf16) for value in (acts, gate, cot, codes)]
        + [pltpu.VMEM(value.shape, value.dtype) for value in constants]
        + [
            pltpu.VMEM((channels * 2 * SUB, LANES), f32),
            pltpu.VMEM((channels * SUB, LANES), f32),
            pltpu.VMEM((channels, 2 * SUB, LANES), bf16),
            pltpu.VMEM((1, LANES), f32),
            pltpu.VMEM((channels, 2 * SUB, LANES), bf16),
            pltpu.VMEM((seqs, SUB, LANES), f32),
            pltpu.VMEM((dps, 1, LANES), f32),
            pltpu.VMEM((1, LANES), f32),
            pltpu.VMEM((seqs, 1, LANES), f32),
            pltpu.VMEM((ROWS, 2 * LANES), f32),
            pltpu.VMEM((dps, seqs, 2 * SUB, LANES), bf16),
            pltpu.VMEM((seqs, SUB, LANES), f32),
            pltpu.VMEM((1, LANES), f32),
            pltpu.VMEM((2 * seqs, SUB, LANES), f32),
            pltpu.VMEM((2 * seqs, 1, LANES), f32),
            pltpu.VMEM((seqs, 2 * SUB, LANES), bf16),
            pltpu.SemaphoreType.DMA((DATA + pairs,)),
            pltpu.SemaphoreType.DMA((DATA + pairs,)),
            pltpu.SemaphoreType.DMA((3,)),
            pltpu.SemaphoreType.DMA((9,)),
            pltpu.SemaphoreType.REGULAR,
        ],
        compiler_params=pltpu.CompilerParams(collective_id=0, has_side_effects=True, vmem_limit_bytes=62 << 20),
    )(acts, gate, cot, codes, filter_scales, first, last, forward_table, backward_table, twist)


def finish_kernel(dps, block, back_ref, grad_ref, rms_ref, cot_ref, filter_scale_ref, input_ref, gate_ref, code_ref, turned, turned_grad):
    lane = lax.broadcasted_iota(jnp.int32, (1, LANES), 1)
    base = lax.axis_index("dp") * (LANES // dps)

    def decode(i, carry):
        at = pl.ds(i * block, block)
        rms = rms_ref[at]
        tile = back_ref[at].astype(jnp.float32)
        conv = root_of(tile[:, :SUB], 14) * (lane_of(rms, lane, base + CONV_LANE) * (1.0 / TOP14))
        back = root_of(tile[:, SUB:], 8) * (lane_of(rms, lane, base + BACK_LANE) * (1.0 / TOP8_RMS))
        rows = pl.ds(pl.multiple_of(i * block * 2 * SUB, 2 * SUB), block * 2 * SUB)
        turned[rows] = jnp.concatenate([conv, back], axis=1).reshape(block * 2 * SUB, LANES)
        grad = grad_ref[pl.ds(i * (block // 2), block // 2)].astype(jnp.float32).reshape(block, SUB, LANES)
        grad = root_of(grad, 8) * (lane_of(rms, lane, GRAD_LANE) * (1.0 / TOP8_RMS))
        turned_grad[pl.ds(pl.multiple_of(i * block * SUB, SUB), block * SUB)] = grad.reshape(block * SUB, LANES)
        return carry

    lax.fori_loop(0, LANES // block, decode, 0)
    for i in range(SUB):
        rows = slice(i * LANES, (i + 1) * LANES)
        conv = turned[pl.ds(i, LANES, stride=2 * SUB)].T
        gate_ref[rows] = (cot_ref[rows].astype(jnp.float32) * conv).astype(jnp.bfloat16)
        input_ref[rows] = turned[pl.ds(SUB + i, LANES, stride=2 * SUB)].T
        code_ref[rows] = turned_grad[pl.ds(i, LANES, stride=SUB)].T * filter_scale_ref[i : i + 1]


def finish(dps, back, grad, rms, cot, filter_scales):
    positions, channels = cot.shape
    part = pl.BlockSpec((positions, LANES), lambda i: (0, i))
    return pl.pallas_call(
        functools.partial(finish_kernel, dps, BLOCK),
        grid=(channels // LANES,),
        out_shape=(
            jax.ShapeDtypeStruct(cot.shape, jnp.float32),
            jax.ShapeDtypeStruct(cot.shape, jnp.bfloat16),
            jax.ShapeDtypeStruct(cot.shape, jnp.float32),
        ),
        in_specs=[
            pl.BlockSpec((LANES, 2 * SUB, LANES), lambda i: (i, 0, 0)),
            pl.BlockSpec((LANES // 2, 2 * SUB, LANES), lambda i: (i, 0, 0)),
            pl.BlockSpec((LANES, 1, LANES), lambda i: (i, 0, 0)),
            part,
            pl.BlockSpec((SUB, LANES), lambda i: (0, i)),
        ],
        out_specs=(part,) * 3,
        scratch_shapes=[
            pltpu.VMEM((LANES * 2 * SUB, LANES), jnp.float32),
            pltpu.VMEM((LANES * SUB, LANES), jnp.float32),
        ],
        compiler_params=pltpu.CompilerParams(vmem_limit_bytes=62 << 20),
    )(back, grad, rms, cot, filter_scales)


def on_device(activations, gate_values, output_grad, filter_codes, filter_scales):
    seqs, dps = lax.axis_size("seq"), lax.axis_size("dp")
    channels = filter_codes.shape[1]
    back, grad, rms = exchange(
        seqs, dps, activations[0], gate_values[0], output_grad[0], filter_codes, filter_scales
    )
    input_grad, gate_grad, code_grad = finish(
        dps, back, grad.reshape(channels // 2, 2 * SUB, LANES), rms.reshape(channels, 1, LANES), output_grad[0], filter_scales
    )
    return (input_grad[None], gate_grad[None], code_grad)


def solution(mesh):
    in_specs = (
        P("dp", "seq", None),
        P("dp", "seq", None),
        P("dp", "seq", None),
        P("seq", None),
        P("seq", None),
    )
    out_specs = (P("dp", "seq", None), P("dp", "seq", None), P("seq", None))
    return jax.shard_map(on_device, mesh=mesh, in_specs=in_specs, out_specs=out_specs, check_vma=False)
```

```python
import functools

import jax
import jax.numpy as jnp
import numpy as np
from jax import lax
from jax.experimental import pallas as pl
from jax.experimental.pallas import tpu as pltpu
from jax.sharding import PartitionSpec as P

LANES = 128
SUB = 8
ROWS = 256
FLOOR = 2.0**-90
TOP8 = 2.0**15
TOP14 = 2.0
TOP8_RMS = 2.0**7.75
RMS_FLOOR = 2.0**-50


def split_np(table):
    high = np.asarray(table, np.float64).astype(jnp.bfloat16)
    low = (np.asarray(table, np.float64) - high.astype(np.float64)).astype(jnp.bfloat16)
    return high, low


def tables():
    whole = 2 * ROWS * LANES
    rows = np.arange(ROWS, dtype=np.float64)
    lanes = np.arange(LANES, dtype=np.float64)
    outer = 2 * np.pi * (rows[:, None] + 0.5) * rows[None, :] / (2 * ROWS)
    first = np.concatenate([np.cos(outer), -np.sin(outer)], axis=0)
    last = np.concatenate([np.cos(outer.T), -np.sin(outer.T)], axis=1) * (2.0 / whole)
    inner = 2 * np.pi * lanes[:, None] * lanes[None, :] / LANES
    cos, sin = np.cos(inner), np.sin(inner)
    forward = np.block([[cos, -sin], [sin, cos]])
    backward = np.block([[cos, sin], [-sin, cos]])
    turn = 2 * np.pi * (rows[:, None] + 0.5) * lanes[None, :] / whole
    twist = np.stack([np.cos(turn), -np.sin(turn)]).astype(np.float32)
    first_hi, first_lo = split_np(first)
    last_hi, last_lo = split_np(last)
    return (
        np.concatenate([first_hi, first_lo], axis=0),
        np.concatenate([last_hi, last_lo], axis=0),
        np.stack(split_np(forward)),
        np.stack(split_np(backward)),
        twist,
    )


def dot(left, right):
    return jnp.dot(left, right, preferred_element_type=jnp.float32)


def halves(value):
    high = value.astype(jnp.bfloat16)
    low = (value - high.astype(jnp.float32)).astype(jnp.bfloat16)
    return high, low


def left_product(table_ref, high, low):
    count = table_ref.shape[0] // 2
    both = dot(table_ref[...], high)
    total = both[:count] + both[count:]
    if low is not None:
        total = total + dot(table_ref[:count], low)
    return total


def right_product(value, table_ref):
    high, low = halves(value)
    return dot(high, table_ref[0]) + dot(low, table_ref[0]) + dot(high, table_ref[1])


def forward(high, low, first_ref, forward_ref, twist_ref):
    section = left_product(first_ref, high, low)
    cos, sin = twist_ref[0], twist_ref[1]
    out = []
    for start in range(0, high.shape[1], LANES):
        real = section[:ROWS, start : start + LANES]
        imag = section[ROWS:, start : start + LANES]
        turned = jnp.concatenate([real * cos - imag * sin, real * sin + imag * cos], axis=1)
        out.append(right_product(turned, forward_ref))
    return out


def inverse(spectra, last_ref, backward_ref, twist_ref):
    cos, sin = twist_ref[0], twist_ref[1]
    sections = []
    for spec in spectra:
        part = right_product(spec, backward_ref)
        real, imag = part[:, :LANES], part[:, LANES:]
        sections.append(jnp.concatenate([real * cos + imag * sin, imag * cos - real * sin], axis=0))
    high, low = halves(jnp.concatenate(sections, axis=1))
    result = left_product(last_ref, high, low)
    return [result[:, i * LANES : (i + 1) * LANES] for i in range(len(spectra))]


def times(left, right):
    lr, li, rr, ri = left[:, :LANES], left[:, LANES:], right[:, :LANES], right[:, LANES:]
    return jnp.concatenate([lr * rr - li * ri, lr * ri + li * rr], axis=1)


def times_conj(left, right):
    lr, li, rr, ri = left[:, :LANES], left[:, LANES:], right[:, :LANES], right[:, LANES:]
    return jnp.concatenate([lr * rr + li * ri, li * rr - lr * ri], axis=1)


def eighth_power(value):
    two = value * value
    four = two * two
    return four * two * value * jnp.abs(value)


def fourteenth_power(value):
    two = value * value
    four = two * two
    return four * four * four * value * jnp.abs(value)


def root_of(code, power):
    size = jnp.exp2(jnp.log2(jnp.abs(code)) * (1.0 / power))
    return jnp.where(code < 0, -size, size)


def root_mean_square(spec):
    whole = 2 * ROWS * LANES
    return jnp.sqrt(jnp.sum(spec * spec, keepdims=True) * (2.0 / whole)) * (1.0 / whole) ** 0.5


def to_peer(source, target, send_sem, recv_sem, seq, dp):
    return pltpu.make_async_remote_copy(
        src_ref=source, dst_ref=target, send_sem=send_sem, recv_sem=recv_sem,
        device_id={"seq": seq, "dp": dp}, device_id_type=pl.DeviceIdType.MESH,
    )


def tell(sem, seq, dp):
    pl.semaphore_signal(sem, inc=1, device_id={"seq": seq, "dp": dp}, device_id_type=pl.DeviceIdType.MESH)


SCALE, TAPS, SCALES, GRAD, RMS, BACK, GRAD_Y, RMS_Y, DATA = range(9)
CONV_LANE, GRAD_LANE, BACK_LANE = 0, 4, 8


AHEAD = 3


BLOCK = 32


def lane_of(rows, lane, wanted):
    return jnp.max(jnp.where(lane == wanted, rows, 0.0), axis=-1, keepdims=True)


def main_kernel(
    seqs, dps, acts_hbm, gate_hbm, cot_hbm, codes_hbm, filter_scale_ref,
    first_hbm, last_hbm, forward_hbm, backward_hbm, twist_hbm,
    back_ref, grad_all_ref, rms_all_ref,
    acts_ref, gate_ref, cot_ref, codes_ref, first_ref, last_ref, forward_ref, backward_ref, twist_ref,
    turned, taps_ref, data_ref, scale_ref,
    got, taps_got, scale_got, scale_row, scales_got, cross_ref, out, grad, rms, held, held_rms,
    grad_code, send_sems, recv_sems, local_sems, load_sems, ready,
):
    seq, dp = lax.axis_index("seq"), lax.axis_index("dp")
    mine = dp * seqs + seq
    pairs = dps // 2
    pair, parity = dp // 2, lax.rem(dp, 2)
    next_seq = lax.rem(seq + 1, seqs)
    lane = lax.broadcasted_iota(jnp.int32, (1, LANES), 1)
    group = LANES // dps
    channels = seqs * dps

    loads = [
        pltpu.make_async_copy(source, target, load_sems.at[i])
        for i, (source, target) in enumerate(
            [(cot_hbm, cot_ref), (gate_hbm, gate_ref), (acts_hbm, acts_ref), (codes_hbm, codes_ref),
             (twist_hbm, twist_ref), (first_hbm, first_ref), (forward_hbm, forward_ref),
             (backward_hbm, backward_ref), (last_hbm, last_ref)]
        )
    ]
    for load in loads:
        load.start()

    def turn():
        for load in loads[:4]:
            load.wait()

        def chunk(i, top):
            at = pl.ds(pl.multiple_of(i * LANES, LANES), LANES)
            acts = acts_ref[at].astype(jnp.float32)
            grads = cot_ref[at].astype(jnp.float32) * gate_ref[at].astype(jnp.float32)
            taps = codes_ref[at].astype(jnp.float32) * filter_scale_ref[pl.ds(i, 1)]
            for start in range(0, channels, LANES):
                part = slice(start, start + LANES)
                turned[pl.ds(start * 2 * SUB + i, LANES, stride=2 * SUB)] = acts[:, part].T
                turned[pl.ds(start * 2 * SUB + SUB + i, LANES, stride=2 * SUB)] = grads[:, part].T
                taps_ref[pl.ds(start * SUB + i, LANES, stride=SUB)] = taps[:, part].T
            return jnp.maximum(top, jnp.max(jnp.abs(grads), axis=0, keepdims=True))

        top = lax.fori_loop(0, SUB, chunk, jnp.zeros((1, channels), jnp.float32))
        top = jnp.maximum(jnp.max(top, keepdims=True), FLOOR)
        scale_ref[...] = jnp.broadcast_to(top * (1.0 / TOP8), (1, LANES))
        factor = (TOP8 / top).reshape(1, 1, 1)

        def code(i, carry):
            tile = turned[pl.ds(pl.multiple_of(i * seqs * 2 * SUB, 2 * SUB), seqs * 2 * SUB)]
            tile = tile.reshape(seqs, 2 * SUB, LANES)
            coded = jnp.concatenate([tile[:, :SUB], eighth_power(tile[:, SUB:] * factor)], axis=1)
            data_ref[pl.ds(i * seqs, seqs)] = coded.astype(jnp.bfloat16)
            return carry

        lax.fori_loop(0, dps, code, 0)

    def copy_to(source, target, kind, seq_to, dp_to, recv_kind=None):
        return to_peer(
            source, target, send_sems.at[kind], recv_sems.at[kind if recv_kind is None else recv_kind], seq_to, dp_to
        )

    def of(ref, count, kind, recv_kind=None):
        part = ref.at[pl.ds(0, count)]
        return copy_to(part, part, kind, next_seq, dp, recv_kind)

    def taps_of(seq_to, dp_to):
        return taps_ref.at[pl.ds(pl.multiple_of((dp_to * seqs + seq_to) * SUB, SUB), SUB)]

    barrier = pltpu.get_barrier_semaphore()

    def tell_pair(offset, carry):
        tell(barrier, lax.rem(seq + offset // 2, seqs), pair * 2 + lax.rem(parity + offset, 2))
        return carry

    def tell_others(sem):
        def body(offset, carry):
            tell(sem, seq, lax.rem(pair + offset, pairs) * 2 + parity)
            return carry

        return body

    lax.fori_loop(1, pairs, tell_others(barrier), 0)
    lax.fori_loop(1, 2 * seqs, tell_pair, 0)
    turn()
    pl.semaphore_wait(barrier, 2 * seqs + pairs - 2)
    lax.fori_loop(1, pairs, tell_others(ready), 0)

    def send_scale(offset, carry):
        copy_to(scale_ref, scale_got.at[dp], SCALE, seq, lax.rem(dp + offset, dps)).start()
        return carry

    def send_taps(offset, carry):
        peer = lax.rem(seq + offset, seqs)
        apart = lax.rem(seq // 2, 4) - lax.rem(peer // 2, 4)
        dp_to = pair * 2 + lax.rem(parity + apart * apart // 9, 2)
        copy_to(taps_of(peer, dp_to), taps_got.at[seq], TAPS, peer, dp_to).start()
        return carry

    lax.fori_loop(1, seqs, send_taps, 0)

    def send_pair(step, source_of, target, kind, recv_kind):
        peer_pair = lax.rem(pair + step, pairs)

        def send(offset, carry):
            peer_seq = lax.rem(seq + offset // 2, seqs)
            peer_dp = peer_pair * 2 + lax.rem(parity + offset, 2)
            copy_to(source_of(peer_seq, peer_dp), target.at[mine], kind, peer_seq, peer_dp, recv_kind).start()
            return carry

        lax.fori_loop(jnp.where(lax.rem(step, pairs) == 0, 1, 0), 2 * seqs, send, 0)

    def send_data(step):
        send_pair(step, lambda s, d: data_ref.at[d * seqs + s], got, DATA + step, DATA + pair)

    def sent_data(step, count):
        of(got, count, DATA + step, DATA + step).wait_send()

    send_data(0)
    pl.semaphore_wait(ready, pairs - 1)
    lax.fori_loop(1, dps, send_scale, 0)
    lax.fori_loop(1, AHEAD, lambda step, carry: (send_data(step), carry)[1], 0)
    own = pltpu.make_async_copy(data_ref.at[mine], got.at[mine], local_sems.at[0])
    own.start()
    own_taps = pltpu.make_async_copy(taps_of(seq, dp), taps_got.at[seq], local_sems.at[1])
    own_taps.start()

    of(scale_got, dps - 1, SCALE).wait()
    scale_got[dp] = scale_ref[...]
    row = jnp.zeros((1, LANES), jnp.float32)
    for other in range(dps):
        row = jnp.where(lane // group == other, scale_got[other], row)
    scale_row[...] = row

    def send_row(offset, carry):
        copy_to(scale_row, scales_got.at[seq], SCALES, lax.rem(seq + offset, seqs), dp).start()
        return carry

    lax.fori_loop(1, seqs, send_row, 0)

    for load in loads[4:]:
        load.wait()
    own_taps.wait()
    of(taps_got, seqs - 1, TAPS).wait()
    taps_high, taps_low = halves(taps_got[...].reshape(ROWS, LANES))
    (taps_spec,) = forward(taps_high, taps_low, first_ref, forward_ref, twist_ref)
    cross_ref[...] = jnp.zeros_like(cross_ref)
    own.wait()
    of(scales_got, seqs - 1, SCALES).wait()
    scales_got[seq] = scale_row[...]
    of(got, 2 * seqs - 1, DATA, DATA + pair).wait_recv()
    rms[...] = jnp.zeros_like(rms)

    def send_back(step):
        send_pair(pairs - step, lambda s, d: out.at[d, s], back_ref, BACK, BACK)

    def send_grads():
        cross = cross_ref[...]
        grad_rms = jnp.maximum(root_mean_square(cross), RMS_FLOOR)
        in_group = lane % group
        rms[...] = jnp.where((in_group >= GRAD_LANE) & (in_group < BACK_LANE), grad_rms, rms[...])
        (grad_value,) = inverse([cross], last_ref, backward_ref, twist_ref)
        grad[...] = grad_value.reshape(seqs, SUB, LANES)

        def send_grad(offset, carry):
            peer_seq = lax.rem(seq + offset // 2, seqs)
            peer_dp = pair * 2 + lax.rem(parity + offset, 2)
            copy_to(grad.at[peer_seq], held.at[parity * seqs + seq], GRAD, peer_seq, peer_dp).start()
            copy_to(rms, held_rms.at[parity * seqs + seq], RMS, peer_seq, peer_dp).start()
            return carry

        lax.fori_loop(1, 2 * seqs, send_grad, 0)

    def transform_pair(step, carry):
        source = lax.rem(pair + pairs - step, pairs)

        @pl.when(step > 0)
        def _():
            of(got, 2 * seqs, DATA, DATA + source).wait_recv()

        @pl.when(step == 0)
        def _():
            sent_data(step, 2 * seqs - 1)

        @pl.when(step < pairs - AHEAD)
        def _():
            send_data(step + AHEAD)

        signals, acts = [], []
        for half in range(2):
            index = source * 2 + half
            tile = got[pl.ds(index * seqs, seqs)].astype(jnp.float32)
            signals.append(tile[:, :SUB].reshape(ROWS, LANES).astype(jnp.bfloat16))
            scale = lane_of(scales_got[...], lane, index * group)
            acts.append((root_of(tile[:, SUB:], 8) * scale).reshape(ROWS, LANES))
        act_high, act_low = halves(jnp.concatenate(acts, axis=1))
        signal_specs = forward(jnp.concatenate(signals, axis=1), None, first_ref, forward_ref, twist_ref)
        act_specs = forward(act_high, act_low, first_ref, forward_ref, twist_ref)
        conv_specs, back_specs, factors = [], [], []
        for half, (signal_spec, act_spec) in enumerate(zip(signal_specs, act_specs)):
            index = source * 2 + half
            cross_ref[...] += times_conj(act_spec, signal_spec)
            conv_spec, back_spec = times(signal_spec, carry), times_conj(act_spec, carry)
            conv_specs.append(conv_spec)
            back_specs.append(back_spec)
            conv_rms = jnp.maximum(root_mean_square(conv_spec), RMS_FLOOR)
            back_rms = jnp.maximum(root_mean_square(back_spec), RMS_FLOOR)
            factors.append((TOP14 / conv_rms, TOP8_RMS / back_rms))
            both = jnp.where(lane % group < BACK_LANE, conv_rms, back_rms)
            rms[...] = jnp.where(lane // group == index, both, rms[...])

        @pl.when(step == pairs - 1)
        def _():
            send_grads()
            send_back(1)
            send_back(2)

        convs = inverse(conv_specs, last_ref, backward_ref, twist_ref)
        backs = inverse(back_specs, last_ref, backward_ref, twist_ref)
        for half in range(2):
            conv_code = fourteenth_power(convs[half] * factors[half][0]).reshape(seqs, SUB, LANES)
            back_code = eighth_power(backs[half] * factors[half][1]).reshape(seqs, SUB, LANES)
            out[source * 2 + half] = jnp.concatenate([conv_code, back_code], axis=1).astype(jnp.bfloat16)

        @pl.when(step == 0)
        def _():
            send_back(step)

        return carry

    lax.fori_loop(0, pairs, transform_pair, taps_spec)
    own_back = pltpu.make_async_copy(out.at[dp, seq], back_ref.at[mine], local_sems.at[0])
    own_back.start()

    of(held, 2 * seqs - 1, GRAD).wait()
    of(held_rms, 2 * seqs - 1, RMS).wait()
    held[parity * seqs + seq] = grad[seq]
    held_rms[parity * seqs + seq] = rms[...]
    code = eighth_power(held[...] * (TOP8_RMS / lane_of(held_rms[...], lane, GRAD_LANE)))
    grad_code[...] = code.reshape(seqs, 2 * SUB, LANES).astype(jnp.bfloat16)

    def send_along(offset, carry):
        peer_dp = lax.rem(pair + offset, pairs) * 2 + parity
        copy_to(grad_code, grad_all_ref.at[pair], GRAD_Y, seq, peer_dp).start()
        copy_to(held_rms, rms_all_ref.at[pair], RMS_Y, seq, peer_dp).start()
        return carry

    lax.fori_loop(1, pairs, send_along, 0)
    lax.fori_loop(3, pairs, lambda step, carry: (send_back(step), carry)[1], 0)
    own_grad = pltpu.make_async_copy(grad_code, grad_all_ref.at[pair], local_sems.at[1])
    own_grad.start()
    own_rms = pltpu.make_async_copy(held_rms, rms_all_ref.at[pair], local_sems.at[2])
    own_rms.start()
    own_back.wait()
    own_grad.wait()
    own_rms.wait()
    lax.fori_loop(pairs - AHEAD, pairs, lambda step, carry: (sent_data(step, 2 * seqs), carry)[1], 0)
    of(grad_all_ref, pairs - 1, GRAD_Y).wait()
    of(rms_all_ref, pairs - 1, RMS_Y).wait()
    of(back_ref, channels - 1, BACK).wait()


def exchange(seqs, dps, acts, gate, cot, codes, filter_scales):
    pairs, channels = dps // 2, seqs * dps
    vmem, hbm = pl.BlockSpec(memory_space=pltpu.VMEM), pl.BlockSpec(memory_space=pl.ANY)
    f32, bf16 = jnp.float32, jnp.bfloat16
    constants = [jnp.asarray(t) for t in tables()]
    first, last, forward_table, backward_table, twist = constants
    return pl.pallas_call(
        functools.partial(main_kernel, seqs, dps),
        out_shape=(
            jax.ShapeDtypeStruct((channels, 2 * SUB, LANES), bf16),
            jax.ShapeDtypeStruct((pairs, seqs, 2 * SUB, LANES), bf16),
            jax.ShapeDtypeStruct((pairs, 2 * seqs, 1, LANES), f32),
        ),
        in_specs=[hbm] * 4 + [vmem] + [hbm] * 5,
        out_specs=(vmem,) * 3,
        scratch_shapes=[pltpu.VMEM(value.shape, bf16) for value in (acts, gate, cot, codes)]
        + [pltpu.VMEM(value.shape, value.dtype) for value in constants]
        + [
            pltpu.VMEM((channels * 2 * SUB, LANES), f32),
            pltpu.VMEM((channels * SUB, LANES), f32),
            pltpu.VMEM((channels, 2 * SUB, LANES), bf16),
            pltpu.VMEM((1, LANES), f32),
            pltpu.VMEM((channels, 2 * SUB, LANES), bf16),
            pltpu.VMEM((seqs, SUB, LANES), f32),
            pltpu.VMEM((dps, 1, LANES), f32),
            pltpu.VMEM((1, LANES), f32),
            pltpu.VMEM((seqs, 1, LANES), f32),
            pltpu.VMEM((ROWS, 2 * LANES), f32),
            pltpu.VMEM((dps, seqs, 2 * SUB, LANES), bf16),
            pltpu.VMEM((seqs, SUB, LANES), f32),
            pltpu.VMEM((1, LANES), f32),
            pltpu.VMEM((2 * seqs, SUB, LANES), f32),
            pltpu.VMEM((2 * seqs, 1, LANES), f32),
            pltpu.VMEM((seqs, 2 * SUB, LANES), bf16),
            pltpu.SemaphoreType.DMA((DATA + pairs,)),
            pltpu.SemaphoreType.DMA((DATA + pairs,)),
            pltpu.SemaphoreType.DMA((3,)),
            pltpu.SemaphoreType.DMA((9,)),
            pltpu.SemaphoreType.REGULAR,
        ],
        compiler_params=pltpu.CompilerParams(collective_id=0, has_side_effects=True, vmem_limit_bytes=62 << 20),
    )(acts, gate, cot, codes, filter_scales, first, last, forward_table, backward_table, twist)


def finish_kernel(dps, block, back_ref, grad_ref, rms_ref, cot_ref, filter_scale_ref, input_ref, gate_ref, code_ref, turned, turned_grad):
    lane = lax.broadcasted_iota(jnp.int32, (1, LANES), 1)
    base = lax.axis_index("dp") * (LANES // dps)

    def decode(i, carry):
        at = pl.ds(i * block, block)
        rms = rms_ref[at]
        tile = back_ref[at].astype(jnp.float32)
        conv = root_of(tile[:, :SUB], 14) * (lane_of(rms, lane, base + CONV_LANE) * (1.0 / TOP14))
        back = root_of(tile[:, SUB:], 8) * (lane_of(rms, lane, base + BACK_LANE) * (1.0 / TOP8_RMS))
        rows = pl.ds(pl.multiple_of(i * block * 2 * SUB, 2 * SUB), block * 2 * SUB)
        turned[rows] = jnp.concatenate([conv, back], axis=1).reshape(block * 2 * SUB, LANES)
        grad = grad_ref[pl.ds(i * (block // 2), block // 2)].astype(jnp.float32).reshape(block, SUB, LANES)
        grad = root_of(grad, 8) * (lane_of(rms, lane, GRAD_LANE) * (1.0 / TOP8_RMS))
        turned_grad[pl.ds(pl.multiple_of(i * block * SUB, SUB), block * SUB)] = grad.reshape(block * SUB, LANES)
        return carry

    lax.fori_loop(0, LANES // block, decode, 0)
    for i in range(SUB):
        rows = slice(i * LANES, (i + 1) * LANES)
        conv = turned[pl.ds(i, LANES, stride=2 * SUB)].T
        gate_ref[rows] = (cot_ref[rows].astype(jnp.float32) * conv).astype(jnp.bfloat16)
        input_ref[rows] = turned[pl.ds(SUB + i, LANES, stride=2 * SUB)].T
        code_ref[rows] = turned_grad[pl.ds(i, LANES, stride=SUB)].T * filter_scale_ref[i : i + 1]


def finish(dps, back, grad, rms, cot, filter_scales):
    positions, channels = cot.shape
    part = pl.BlockSpec((positions, LANES), lambda i: (0, i))
    return pl.pallas_call(
        functools.partial(finish_kernel, dps, BLOCK),
        grid=(channels // LANES,),
        out_shape=(
            jax.ShapeDtypeStruct(cot.shape, jnp.float32),
            jax.ShapeDtypeStruct(cot.shape, jnp.bfloat16),
            jax.ShapeDtypeStruct(cot.shape, jnp.float32),
        ),
        in_specs=[
            pl.BlockSpec((LANES, 2 * SUB, LANES), lambda i: (i, 0, 0)),
            pl.BlockSpec((LANES // 2, 2 * SUB, LANES), lambda i: (i, 0, 0)),
            pl.BlockSpec((LANES, 1, LANES), lambda i: (i, 0, 0)),
            part,
            pl.BlockSpec((SUB, LANES), lambda i: (0, i)),
        ],
        out_specs=(part,) * 3,
        scratch_shapes=[
            pltpu.VMEM((LANES * 2 * SUB, LANES), jnp.float32),
            pltpu.VMEM((LANES * SUB, LANES), jnp.float32),
        ],
        compiler_params=pltpu.CompilerParams(vmem_limit_bytes=62 << 20),
    )(back, grad, rms, cot, filter_scales)


def on_device(activations, gate_values, output_grad, filter_codes, filter_scales):
    seqs, dps = lax.axis_size("seq"), lax.axis_size("dp")
    channels = filter_codes.shape[1]
    back, grad, rms = exchange(
        seqs, dps, activations[0], gate_values[0], output_grad[0], filter_codes, filter_scales
    )
    input_grad, gate_grad, code_grad = finish(
        dps, back, grad.reshape(channels // 2, 2 * SUB, LANES), rms.reshape(channels, 1, LANES), output_grad[0], filter_scales
    )
    return (input_grad[None], gate_grad[None], code_grad)


def solution(mesh):
    in_specs = (
        P("dp", "seq", None),
        P("dp", "seq", None),
        P("dp", "seq", None),
        P("seq", None),
        P("seq", None),
    )
    out_specs = (P("dp", "seq", None), P("dp", "seq", None), P("seq", None))
    return jax.shard_map(on_device, mesh=mesh, in_specs=in_specs, out_specs=out_specs, check_vma=False)
```
